256 devices in a mesh: rep: 16 (over x, z_lo, core), shard: 16 (over y, z_hi).
Axes of the slice: x: 4, y: 4, z: 8 (z_hi: 4, z_lo: 2; z = z_hi * 2 + z_lo), core: 2. Of those that a mesh axis runs over, the one named last changes fastest.
Arguments:
- hidden: bfloat16 [16, 4096, 8192], P('rep', 'shard'), may hold values from -6 to 6
- cotangent: bfloat16 [16, 4096, 512], P('rep', 'shard'), may hold values from -48 to 48
- norm_gain: float32 [8192], replicated, may hold values from 0.1 to 1.9
- params: float32 [16, 8192, 512], P('rep', 'shard'), may hold values from -6 to 6
- adam_first: float32 [16, 8192, 512], P('rep', 'shard'), may hold values from -4 to 4
- adam_second: float32 [16, 8192, 512], P('rep', 'shard'), may hold values from 0.25 to 4
- outer_anchor: float32 [16, 16, 32, 512], P('shard', 'rep'), may hold values from -6 to 6
- outer_momentum: float32 [16, 16, 32, 512], P('shard', 'rep'), may hold values from -4 to 4
- fragment: int32 [], replicated, may hold values from 0 to 3
- inner_step: int32 [], replicated, may hold values from 1 to 2048
Outputs:
- value_rows: bfloat16 [16, 4096, 512], P('rep', 'shard')
- new_params: float32 [16, 8192, 512], P('rep', 'shard')
- new_first: float32 [16, 8192, 512], P('rep', 'shard')
- new_second: float32 [16, 8192, 512], P('rep', 'shard')
- new_anchor: float32 [16, 16, 32, 512], P('shard', 'rep')
- new_momentum: float32 [16, 16, 32, 512], P('shard', 'rep')
The draws below stay inside these ranges and needn't reach their ends.
All inputs are finite; a program needn't handle non-finite values.
Results may differ from the reference program's by a relative error of at most 0.0048.
The reference program's roundings to bfloat16 on the way (of `normed` and `weights_half`) count: a program that leaves them out, or rounds other values in their place, can miss the bound.
Values may be sent and summed in bfloat16 or wider, within the bound.
No kernel may reach another device: no remote copies, remote signals or barrier semaphores. Data moves between devices by JAX's collectives and lax.ppermute only.
A program may use at most 128 MiB of HBM per device.

```python
import math
import jax
import jax.numpy as jnp
from jax import lax

D = 8192
VCOLS = 512
FRAG = 4
FCOLS = 128
REP_TOK = 4096
OROWS = 32
N_REP = 16
N_SHARD = 16


def steps_of(own_key, dims, shards, least, high):
    def one(dim, shards_of):
        steps = jax.random.uniform(jax.random.fold_in(jax.random.fold_in(own_key, 6), dim), (shards_of,), jnp.float32, least / len(shards), high / len(shards))
        return jnp.repeat(jnp.exp(steps), dims[dim] // shards_of).reshape((-1,) + (1,) * (len(dims) - dim - 1))

    level = one(*shards[0])
    for cut in shards[1:]:
        level = level * one(*cut)
    return level


def scatter_about(key, shape, deviation, bound, cuts=(), held_as=jnp.bfloat16):
    array = deviation * jax.random.normal(key, shape, jnp.float32)
    if cuts:
        array = array * steps_of(key, shape, cuts, -0.22, 0.18)
    return jnp.clip(array, -bound, bound).astype(held_as)


def setup_inputs(seed: int = 0) -> dict:
    seeds = jax.random.split(jax.random.key(seed), 11)
    return {
        "hidden": scatter_about(seeds[0], (N_REP, REP_TOK, D), 1.0, 6.0, ((0, 16), (1, 16))),
        "cotangent": scatter_about(seeds[1], (N_REP, REP_TOK, VCOLS), 8.0, 48.0, ((0, 16), (1, 16))),
        "norm_gain": jnp.clip(1.0 + 0.18 * jax.random.normal(seeds[2], (D,), jnp.float32), 0.1, 1.9),
        "params": scatter_about(seeds[3], (N_REP, D, VCOLS), 1.0, 6.0, ((0, 16), (1, 16)), jnp.float32),
        "adam_first": scatter_about(seeds[4], (N_REP, D, VCOLS), 0.5, 4.0, ((0, 16), (1, 16)), jnp.float32),
        "adam_second": jnp.clip(jnp.exp(math.log(4.0) - 2.7725887 * jax.random.uniform(seeds[5], (N_REP, D, VCOLS), jnp.float32) ** steps_of(seeds[5], (N_REP, D, VCOLS), ((0, 16), (1, 16)), -0.2, 0.2)), 0.25, 4.0),
        "outer_anchor": scatter_about(seeds[6], (N_SHARD, N_REP, OROWS, VCOLS), 1.0, 6.0, ((0, 16), (1, 16)), jnp.float32),
        "outer_momentum": scatter_about(seeds[7], (N_SHARD, N_REP, OROWS, VCOLS), 0.5, 4.0, ((0, 16), (1, 16)), jnp.float32),
        "fragment": jax.random.randint(seeds[8], (), 0, FRAG).astype(jnp.int32),
        "inner_step": jax.random.randint(seeds[9], (), 1, 2049).astype(jnp.int32),
    }


FIRST_DECAY = 0.9
SECOND_DECAY = 0.95
ADAM_EPSILON = 1e-08
PEAK_RATE = 0.125
WEIGHT_DECAY = 0.1
HORIZON_STEPS = 4096.0
OUTER_RATE = 0.7
OUTER_MOMENTUM = 0.9
NORM_EPSILON = 1e-05

def normalise(rows, gain):
    widened = rows.astype(jnp.float32)
    spread = lax.optimization_barrier(jnp.mean(widened * widened, axis=-1, keepdims=True))
    return (widened * lax.rsqrt(spread + NORM_EPSILON) * gain).astype(jnp.bfloat16)

def adam_update(weights, gradient, first, second, inner_step):
    clock = inner_step.astype(jnp.float32)
    rate = PEAK_RATE * 0.5 * (1.0 + jnp.cos(math.pi * clock / HORIZON_STEPS))
    first_corr = 1.0 - jnp.power(FIRST_DECAY, clock)
    second_corr = 1.0 - jnp.power(SECOND_DECAY, clock)
    first_new = FIRST_DECAY * first + (1.0 - FIRST_DECAY) * gradient
    second_new = SECOND_DECAY * second + (1.0 - SECOND_DECAY) * gradient * gradient
    update = first_new / first_corr / (jnp.sqrt(second_new / second_corr) + ADAM_EPSILON)
    stepped = weights - rate * (update + WEIGHT_DECAY * weights)
    return (stepped, first_new, second_new)

def reference(hidden, cotangent, norm_gain, params, adam_first, adam_second, outer_anchor, outer_momentum, fragment, inner_step):
    factor = D ** (-0.5)
    columns = jnp.arange(VCOLS, dtype=jnp.int32)
    in_frag = columns // FCOLS == fragment
    anchor = outer_anchor.reshape(D, VCOLS)
    momentum = outer_momentum.reshape(D, VCOLS)
    mean_params = lax.optimization_barrier(jnp.sum(params, axis=0)) / N_REP
    delta = anchor - mean_params
    momentum_next = jnp.where(in_frag, OUTER_MOMENTUM * momentum + delta, momentum)
    anchor_next = jnp.where(in_frag, anchor - OUTER_RATE * (delta + OUTER_MOMENTUM * momentum_next), anchor)
    values_all = []
    params_all = []
    first_all = []
    second_all = []
    for replica in range(N_REP):
        normed = normalise(hidden[replica], norm_gain)
        weights_half = params[replica].astype(jnp.bfloat16)
        values_all.append((jnp.dot(normed, weights_half, preferred_element_type=jnp.float32) * factor).astype(jnp.bfloat16))
        gradient = jnp.dot(normed.T, cotangent[replica], preferred_element_type=jnp.float32) * factor
        stepped, first_new, second_new = adam_update(params[replica], gradient, adam_first[replica], adam_second[replica], inner_step)
        params_all.append(jnp.where(in_frag, anchor_next + (stepped - params[replica]), stepped))
        first_all.append(first_new)
        second_all.append(second_new)
    blocked = (N_SHARD, N_REP, OROWS, VCOLS)
    return (jnp.stack(values_all), jnp.stack(params_all), jnp.stack(first_all), jnp.stack(second_all), anchor_next.reshape(blocked), momentum_next.reshape(blocked))
```

```python
import functools
import math

import jax
import jax.numpy as jnp
from jax import lax
from jax.experimental import pallas as pl
from jax.experimental.pallas import tpu as pltpu
from jax.sharding import PartitionSpec as P

FRAG = 4
RING = 4
CHUNKS = 2

FIRST_DECAY = 0.9
SECOND_DECAY = 0.95
ADAM_EPSILON = 1e-08
PEAK_RATE = 0.125
WEIGHT_DECAY = 0.1
HORIZON_STEPS = 4096.0
OUTER_RATE = 0.7
OUTER_MOMENTUM = 0.9
NORM_EPSILON = 1e-05

VMEM_LIMIT = 50 * 1024 * 1024
F32 = jnp.float32
BF16 = jnp.bfloat16


def shift_y(array, k):
    pairs = [(y * RING + z, (y + k) % RING * RING + z) for y in range(RING) for z in range(RING)]
    return lax.ppermute(array, "shard", pairs)


def shift_z(array, k):
    pairs = [(y * RING + z, y * RING + (z + k) % RING) for y in range(RING) for z in range(RING)]
    return lax.ppermute(array, "shard", pairs)


def swap_rep(array, bit):
    return lax.ppermute(array, "rep", [(r, r ^ bit) for r in range(16)])


def shift_x(array, k):
    return lax.ppermute(array, "rep", [(r, (r + 4 * k) % 16) for r in range(16)])


def whole(n):
    return [pl.BlockSpec(memory_space=pltpu.VMEM)] * n


def scalars():
    return pl.BlockSpec(memory_space=pltpu.SMEM)


def params_of():
    return pltpu.CompilerParams(vmem_limit_bytes=VMEM_LIMIT)


def pack_kernel(place, hidden_ref, gain_ref, *outs):
    y, z = place[0], place[1]
    features = hidden_ref.shape[1]
    group = features // RING
    width = group // RING // CHUNKS
    widened = hidden_ref[...].astype(F32)
    scale = lax.rsqrt(jnp.mean(widened * widened, axis=-1, keepdims=True) + NORM_EPSILON)
    for chunk in range(CHUNKS):
        for ky in range(RING):
            for kz in range(RING):
                start = lax.rem(y + ky, RING) * group + lax.rem(z + RING - kz, RING) * (group // RING) + chunk * width
                columns = pl.ds(pl.multiple_of(start, width), width)
                block = hidden_ref[:, columns].astype(F32) * scale * gain_ref[:, columns]
                outs[chunk * RING + ky][:, kz * width : (kz + 1) * width] = block.astype(BF16)


def pack(place, hidden, gain):
    tokens, features = hidden.shape
    rows = 32
    width = features // RING // CHUNKS
    outs = CHUNKS * RING
    flat = pl.pallas_call(
        pack_kernel,
        out_shape=[jax.ShapeDtypeStruct((tokens, width), BF16)] * outs,
        grid_spec=pltpu.PrefetchScalarGridSpec(
            num_scalar_prefetch=1,
            grid=(tokens // rows,),
            in_specs=[
                pl.BlockSpec((rows, features), lambda i, place: (i, 0)),
                pl.BlockSpec((1, features), lambda i, place: (0, 0)),
            ],
            out_specs=[pl.BlockSpec((rows, width), lambda i, place: (i, 0))] * outs,
        ),
        compiler_params=params_of(),
        cost_estimate=pl.CostEstimate(flops=0, bytes_accessed=4 * tokens * features, transcendentals=0),
        name="pack",
    )(place, hidden, gain)
    return [flat[c * RING : (c + 1) * RING] for c in range(CHUNKS)]


def gradient_kernel(*refs):
    normed, cot = refs[:RING], refs[RING : 2 * RING]
    own, left, right, keep_left, keep_right = refs[2 * RING :]
    height = own.shape[0]
    half = height // 2
    cot_all = jnp.concatenate([c[...] for c in cot], axis=0)

    def block(kz):
        rows = jnp.concatenate([n[:, kz * height : (kz + 1) * height] for n in normed], axis=0)
        return lax.dot_general(rows, cot_all, (((0,), (0,)), ((), ())), preferred_element_type=F32)

    far = block(2).astype(BF16)
    left[:half] = far[:half]
    right[half:] = far[half:]
    near = block(1)
    keep_left[...] = near[:half]
    left[half:] = near[half:].astype(BF16)
    near = block(3)
    keep_right[...] = near[half:]
    right[:half] = near[:half].astype(BF16)
    own[...] = block(0)


def gradient_chunk(normed, cot):
    tokens, width = normed[0].shape
    columns = cot[0].shape[1]
    height = width // RING
    full, part = (height, columns), (height // 2, columns)
    return pl.pallas_call(
        gradient_kernel,
        out_shape=[
            jax.ShapeDtypeStruct(full, F32),
            jax.ShapeDtypeStruct(full, BF16),
            jax.ShapeDtypeStruct(full, BF16),
            jax.ShapeDtypeStruct(part, F32),
            jax.ShapeDtypeStruct(part, F32),
        ],
        in_specs=whole(2 * RING),
        out_specs=whole(5),
        compiler_params=params_of(),
        cost_estimate=pl.CostEstimate(
            flops=2 * RING * tokens * width * columns, bytes_accessed=2 * RING * tokens * (width + columns) + 8 * width * columns // 4, transcendentals=0
        ),
        name="gradient_chunk",
    )(*normed, *cot)


def values_kernel(*refs):
    n = CHUNKS * RING
    normed = refs[:n]
    own, before, far_top, far_bottom, after = refs[n : n + 5]
    outs = refs[n + 5 :]
    height = own.shape[0]
    step = height // CHUNKS
    half = height // 2
    totals = [None] * RING
    for chunk in range(CHUNKS):
        rows = slice(chunk * step, (chunk + 1) * step)
        if chunk * step < half:
            assert (chunk + 1) * step <= half or CHUNKS == 1
            far = far_top[chunk * step : (chunk + 1) * step]
        else:
            far = far_bottom[chunk * step - half : (chunk + 1) * step - half]
        weights = jnp.concatenate([own[rows], before[rows], far, after[rows]], axis=0)
        for ky in range(RING):
            product = jnp.dot(normed[chunk * RING + ky][...], weights, preferred_element_type=F32)
            totals[ky] = product if chunk == 0 else totals[ky] + product
    for ky in range(RING):
        outs[ky][...] = totals[ky].astype(outs[ky].dtype)


def values_partial(normed, weights):
    tokens, width = normed[0].shape
    columns = weights[0].shape[1]
    return pl.pallas_call(
        values_kernel,
        out_shape=[jax.ShapeDtypeStruct((tokens, columns), F32 if k == 0 else BF16) for k in range(RING)],
        in_specs=whole(len(normed) + 5),
        out_specs=whole(RING),
        compiler_params=params_of(),
        cost_estimate=pl.CostEstimate(
            flops=2 * tokens * width * columns * len(normed), bytes_accessed=2 * tokens * width * len(normed) + 8 * tokens * columns + 8 * 512 * columns, transcendentals=0
        ),
        name="values_partial",
    )(*normed, *weights)


def adam_kernel(place, rates, weights, first, second, *refs):
    pieces = refs[: 5 * CHUNKS]
    anchor_near, anchor_far, out_weights, out_first, out_second = refs[5 * CHUNKS :]
    fragment, rep = place[2], place[3]
    x, zl, core = rep // 4, lax.rem(rep // 2, 2), lax.rem(rep, 2)
    rate, first_scale, second_scale, factor = rates[0], rates[1], rates[2], rates[3]
    step = weights.shape[0] // CHUNKS
    width = weights.shape[1] // FRAG
    for chunk in range(CHUNKS):
        own, from_left, from_right, last_left, last_right = pieces[5 * chunk : 5 * chunk + 5]
        half = step // 2
        for part in range(2):
            if part == 0:
                total = own[:half] + from_right[:half].astype(F32) + last_left[...].astype(F32)
            else:
                total = own[half:] + from_left[half:].astype(F32) + last_right[...].astype(F32)
            rows = slice(chunk * step + part * half, chunk * step + (part + 1) * half)
            gradient = total * factor
            first_new = FIRST_DECAY * first[rows] + (1.0 - FIRST_DECAY) * gradient
            second_new = SECOND_DECAY * second[rows] + (1.0 - SECOND_DECAY) * gradient * gradient
            out_first[rows] = first_new
            out_second[rows] = second_new
            update = (first_new * first_scale) / (jnp.sqrt(second_new * second_scale) + ADAM_EPSILON)
            out_weights[rows] = weights[rows] - rate * (update + WEIGHT_DECAY * weights[rows])
    for q in range(FRAG):

        @pl.when(fragment == q)
        def _():
            columns = slice(q * width, (q + 1) * width)
            for r in range(16):
                rows = slice(r * 32, (r + 1) * 32)
                where = lax.rem(x + 4 - r // 4, 4)
                other = lax.rem(zl + r // 2, 2)
                base = jnp.where(core == r % 2, anchor_near[other * 4 + where], anchor_far[other * 4 + where])
                out_weights[rows, columns] = base + (out_weights[rows, columns] - weights[rows, columns])


def adam(place, rates, weights, first, second, pieces, anchor_near, anchor_far):
    shape = jax.ShapeDtypeStruct(weights.shape, F32)
    return pl.pallas_call(
        adam_kernel,
        out_shape=[shape] * 3,
        in_specs=[scalars(), scalars()] + whole(3 + len(pieces) + 2),
        out_specs=whole(3),
        compiler_params=params_of(),
        cost_estimate=pl.CostEstimate(flops=20 * weights.size, bytes_accessed=32 * weights.size, transcendentals=0),
        name="adam",
    )(place, rates, weights, first, second, *pieces, anchor_near, anchor_far)


def pick(array, index, axis):
    return lax.dynamic_index_in_dim(array, index, axis, keepdims=False)


def local(
    hidden,
    cotangent,
    norm_gain,
    params,
    adam_first,
    adam_second,
    outer_anchor,
    outer_momentum,
    fragment,
    inner_step,
):
    tokens = hidden[0]
    cot_local = cotangent[0]
    weights = params[0]
    factor = tokens.shape[1] ** (-0.5)
    shard = lax.axis_index("shard")
    rep = lax.axis_index("rep")
    place = jnp.stack([shard // RING, shard % RING, fragment, rep]).astype(jnp.int32)

    weights_half = weights.astype(BF16)
    half = weights.shape[0] // 2
    before = shift_z(weights_half, 1)
    after = shift_z(weights_half, -1)
    cot = [cot_local] + [shift_y(cot_local, k) for k in (1, 3, 2)]

    packed = pack(place, tokens, norm_gain.reshape(1, -1))
    normed = []
    for chunk in range(CHUNKS):
        mine = packed[chunk]
        normed.append([mine[0]] + [shift_y(mine[k], k) for k in (1, 3, 2)])
    far_top = shift_z(before[:half], 1)
    far_bottom = shift_z(after[half:], -1)

    frag_width = weights.shape[1] // FRAG
    frag_start = fragment * frag_width
    x, zl, core = rep // 4, rep // 2 % 2, rep % 2
    total = lax.dynamic_slice_in_dim(weights, frag_start, frag_width, 1).reshape(4, 2, 2, -1, frag_width)
    total = pick(total, core, 2) + swap_rep(pick(total, 1 - core, 2), 1)
    total = pick(total, zl, 1) + swap_rep(pick(total, 1 - zl, 1), 2)
    arrived = [shift_x(pick(total, (x + k) % 4, 0), k) for k in (1, 2, 3)]
    total = pick(total, x, 0) + arrived[0] + arrived[1] + arrived[2]
    anchor_local = outer_anchor[0, 0]
    moment_local = outer_momentum[0, 0]
    anchor_frag = lax.dynamic_slice_in_dim(anchor_local, frag_start, frag_width, 1)
    moment_frag = lax.dynamic_slice_in_dim(moment_local, frag_start, frag_width, 1)
    delta = anchor_frag - total / lax.axis_size("rep")
    moment_new = OUTER_MOMENTUM * moment_frag + delta
    anchor_new = anchor_frag - OUTER_RATE * (delta + OUTER_MOMENTUM * moment_new)
    anchor_out = lax.dynamic_update_slice_in_dim(anchor_local, anchor_new, frag_start, 1)
    moment_out = lax.dynamic_update_slice_in_dim(moment_local, moment_new, frag_start, 1)
    near = jnp.stack([anchor_new] + [shift_x(anchor_new, k) for k in (1, 2, 3)])
    near = jnp.concatenate([near, swap_rep(near, 2)])
    far = swap_rep(near, 1)

    pieces = []
    for chunk in range(CHUNKS):
        own, left, right, keep_left, keep_right = gradient_chunk(normed[chunk], cot)
        from_left, from_right = shift_z(left, -1), shift_z(right, 1)
        quarter = from_left.shape[0] // 2
        last_left = (keep_left + from_left[:quarter].astype(F32)).astype(BF16)
        last_right = (keep_right + from_right[quarter:].astype(F32)).astype(BF16)
        pieces += [own, from_left, from_right, shift_z(last_left, -1), shift_z(last_right, 1)]

    partial = values_partial(sum(normed, []), [weights_half, before, far_top, far_bottom, after])
    summed = partial[0]
    for k, source in zip((1, 3, 2), partial[1:]):
        summed = summed + shift_y(source, -k).astype(F32)
    value_rows = (summed * factor).astype(BF16)

    clock = inner_step.astype(F32)
    rate = PEAK_RATE * 0.5 * (1.0 + jnp.cos(math.pi * clock / HORIZON_STEPS))
    first_scale = 1.0 / (1.0 - jnp.power(FIRST_DECAY, clock))
    second_scale = 1.0 / (1.0 - jnp.power(SECOND_DECAY, clock))
    rates = jnp.stack([rate, first_scale, second_scale, jnp.full((), factor, F32)])
    params_out, first_new, second_new = adam(
        place, rates, weights, adam_first[0], adam_second[0], pieces, near, far
    )
    return (
        value_rows[None],
        params_out[None],
        first_new[None],
        second_new[None],
        anchor_out[None, None],
        moment_out[None, None],
    )


def solution(mesh):
    in_specs = (
        P("rep", "shard", None),
        P("rep", "shard", None),
        P(),
        P("rep", "shard", None),
        P("rep", "shard", None),
        P("rep", "shard", None),
        P("shard", "rep", None, None),
        P("shard", "rep", None, None),
        P(),
        P(),
    )
    out_specs = (
        P("rep", "shard", None),
        P("rep", "shard", None),
        P("rep", "shard", None),
        P("rep", "shard", None),
        P("shard", "rep", None, None),
        P("shard", "rep", None, None),
    )
    return jax.shard_map(local, mesh=mesh, in_specs=in_specs, out_specs=out_specs, check_vma=False)
```

```python
import functools
import math

import jax
import jax.numpy as jnp
from jax import lax
from jax.experimental import pallas as pl
from jax.experimental.pallas import tpu as pltpu
from jax.sharding import PartitionSpec as P

FRAG = 4
RING = 4
N_REP = 16
CHUNKS = ((0, 256), (256, 256))

FIRST_DECAY = 0.9
SECOND_DECAY = 0.95
ADAM_EPSILON = 1e-08
PEAK_RATE = 0.125
WEIGHT_DECAY = 0.1
HORIZON_STEPS = 4096.0
OUTER_RATE = 0.7
OUTER_MOMENTUM = 0.9
NORM_EPSILON = 1e-05

COST = pl.CostEstimate(flops=1, bytes_accessed=1, transcendentals=0)
VMEM_LIMIT = 62 * 1024 * 1024
F32 = jnp.float32
BF16 = jnp.bfloat16


def exchange_y(array):
    groups = [[y * RING + z for y in range(RING)] for z in range(RING)]
    return lax.all_to_all(array, "shard", 0, 0, axis_index_groups=groups, tiled=True)


def shift_z(array, k):
    pairs = [(y * RING + z, y * RING + (z + k) % RING) for y in range(RING) for z in range(RING)]
    return lax.ppermute(array, "shard", pairs)


def swap_rep(array, bit):
    return lax.ppermute(array, "rep", [(r, r ^ bit) for r in range(16)])


def shift_y(array, k):
    pairs = [(y * RING + z, (y + k) % RING * RING + z) for y in range(RING) for z in range(RING)]
    return lax.ppermute(array, "shard", pairs)


def whole(n):
    return [pl.BlockSpec(memory_space=pltpu.VMEM)] * n


def scalars():
    return pl.BlockSpec(memory_space=pltpu.SMEM)


def params_of():
    return pltpu.CompilerParams(vmem_limit_bytes=VMEM_LIMIT)


def first_pack_kernel(place, hidden_ref, gain_ref, cot_ref, out, scale_ref):
    z = place[1]
    group = hidden_ref.shape[1] // RING
    block = group // RING
    first, width = CHUNKS[0]
    widened = hidden_ref[...].astype(F32)
    scale = lax.rsqrt(jnp.mean(widened * widened, axis=-1, keepdims=True) + NORM_EPSILON)
    scale_ref[...] = scale
    for y in range(RING):
        for kz in range(RING):
            start = y * group + lax.rem(z + RING - kz, RING) * block + first
            columns = pl.ds(pl.multiple_of(start, 128), width)
            normed = hidden_ref[:, columns].astype(F32) * scale * gain_ref[:, columns]
            out[y, :, kz * width : (kz + 1) * width] = normed.astype(BF16)
        out[y, :, RING * width :] = cot_ref[...]


def first_pack(place, hidden, gain, cot):
    tokens, features = hidden.shape
    columns = cot.shape[1]
    rows = 64
    total = RING * CHUNKS[0][1] + columns
    return pl.pallas_call(
        first_pack_kernel,
        out_shape=[pltpu.HBM((RING, tokens, total), BF16), pltpu.HBM((tokens, 1), F32)],
        grid_spec=pltpu.PrefetchScalarGridSpec(
            num_scalar_prefetch=1,
            grid=(tokens // rows,),
            in_specs=[
                pl.BlockSpec((rows, features), lambda i, place: (i, 0)),
                pl.BlockSpec((1, features), lambda i, place: (0, 0)),
                pl.BlockSpec((rows, columns), lambda i, place: (i, 0)),
            ],
            out_specs=[
                pl.BlockSpec((RING, rows, total), lambda i, place: (0, i, 0)),
                pl.BlockSpec((rows, 1), lambda i, place: (i, 0)),
            ],
        ),
        compiler_params=params_of(),
        cost_estimate=COST,
        name="first_pack",
    )(place, hidden, gain, cot)


def later_pack_kernel(place, *refs):
    hidden, gain, scale = refs[:RING], refs[RING : 2 * RING], refs[2 * RING]
    outs = refs[-RING:]
    for ky in range(RING):
        outs[ky][...] = (hidden[ky][...].astype(F32) * scale[...] * gain[ky][...]).astype(BF16)


def later_pack(place, hidden, gain, scale, after):
    tokens, features = hidden.shape
    first, width = CHUNKS[1]
    per_place = features // RING // RING // width

    def column(ky):
        def at(kz, place):
            whose = lax.rem(place[0] + ky, RING) * RING + lax.rem(place[1] + RING - kz, RING)
            return (0, whose * per_place + first // width)

        return at

    return pl.pallas_call(
        later_pack_kernel,
        out_shape=[pltpu.HBM((tokens, RING * width), BF16)] * RING,
        grid_spec=pltpu.PrefetchScalarGridSpec(
            num_scalar_prefetch=1,
            grid=(RING,),
            in_specs=[pl.BlockSpec((tokens, width), column(ky)) for ky in range(RING)]
            + [pl.BlockSpec((1, width), column(ky)) for ky in range(RING)]
            + [pl.BlockSpec((tokens, 1), lambda kz, place: (0, 0))]
            + [pl.BlockSpec(memory_space=pl.ANY)] * len(after),
            out_specs=[pl.BlockSpec((tokens, width), lambda kz, place: (0, kz))] * RING,
        ),
        compiler_params=params_of(),
        cost_estimate=COST,
        name="later_pack",
    )(place, *[hidden] * RING, *[gain] * RING, scale, *after)


def gradient_block(normed, cot, kz, height):
    rows = jnp.concatenate([n[:, kz * height : (kz + 1) * height] for n in normed], axis=0)
    return lax.dot_general(rows, cot, (((0,), (0,)), ((), ())), preferred_element_type=F32)


def gradient_blocks(normed, cot, own, left, right, keep_left, keep_right):
    height = own.shape[0]
    half = height // 2
    far = gradient_block(normed, cot, 2, height).astype(BF16)
    left[:half] = far[:half]
    right[half:] = far[half:]
    near = gradient_block(normed, cot, 1, height)
    keep_left[...] = near[:half]
    left[half:] = near[half:].astype(BF16)
    near = gradient_block(normed, cot, 3, height)
    keep_right[...] = near[half:]
    right[:half] = near[:half].astype(BF16)
    own[...] = gradient_block(normed, cot, 0, height)


def first_gradient_kernel(normed, cot, *refs):
    rows = [normed.at[y] for y in range(RING)]
    gradient_blocks(rows, jnp.concatenate([cot[y] for y in range(RING)], axis=0), *refs[-5:])


def first_gradient(arrived, after):
    tokens = arrived.shape[1]
    height = CHUNKS[0][1]
    columns = arrived.shape[2] - RING * height
    full, part = (height, columns), (height // 2, columns)
    shapes = [(full, F32), (full, BF16), (full, BF16), (part, F32), (part, F32)]
    cot_at = RING * height // columns
    return pl.pallas_call(
        first_gradient_kernel,
        grid=(1,),
        out_shape=[pltpu.HBM(*s) for s in shapes],
        in_specs=[
            pl.BlockSpec((RING, tokens, RING * height), lambda i: (0, 0, 0)),
            pl.BlockSpec((RING, tokens, columns), lambda i: (0, 0, cot_at)),
        ]
        + [pl.BlockSpec(memory_space=pl.ANY)] * len(after),
        out_specs=[pl.BlockSpec(s[0], lambda i: (0, 0)) for s in shapes],
        compiler_params=params_of(),
        cost_estimate=COST,
        name="first_gradient",
    )(arrived, arrived, *after)


def later_gradient_kernel(place, *refs):
    normed, cot = refs[:RING], refs[RING]
    keep_left, keep_right, from_left, from_right = refs[RING + 1 : RING + 5]
    own, left, right, next_left, next_right = refs[-5:]
    half = keep_left.shape[0]
    left[:half] = (keep_left[...] + from_left[:half].astype(F32)).astype(BF16)
    right[:half] = (keep_right[...] + from_right[half:].astype(F32)).astype(BF16)
    cot_all = jnp.concatenate([cot[lax.rem(place[0] + RING - k, RING)] for k in range(RING)], axis=0)
    gradient_blocks(normed, cot_all, own, left.at[half:], right.at[half:], next_left, next_right)


def later_gradient(place, normed, arrived, kept, after):
    tokens = arrived.shape[1]
    height = CHUNKS[1][1]
    columns = kept[0].shape[1]
    full, part = (height, columns), (height // 2, columns)
    sent = (height + kept[0].shape[0], columns)
    shapes = [(full, F32), (sent, BF16), (sent, BF16), (part, F32), (part, F32)]
    cot_at = RING * CHUNKS[0][1] // columns
    return pl.pallas_call(
        later_gradient_kernel,
        grid=(1,),
        out_shape=[pltpu.HBM(*s) for s in shapes],
        in_specs=[scalars()]
        + [pl.BlockSpec((tokens, RING * height), lambda i: (0, 0))] * RING
        + [pl.BlockSpec((RING, tokens, columns), lambda i: (0, 0, cot_at))]
        + [pl.BlockSpec(k.shape, lambda i: (0, 0)) for k in kept]
        + [pl.BlockSpec(memory_space=pl.ANY)] * len(after),
        out_specs=[pl.BlockSpec(s[0], lambda i: (0, 0)) for s in shapes],
        compiler_params=params_of(),
        cost_estimate=COST,
        name="later_gradient",
    )(place, *normed, arrived, *kept, *after)


def chunk_weights(chunk, own, before, far_top, far_bottom, after):
    first, width = CHUNKS[chunk]
    rows = slice(first, first + width)
    half = far_top.shape[0]
    far = []
    if first < half:
        far.append(far_top[first : min(first + width, half)])
    if first + width > half:
        far.append(far_bottom[max(first - half, 0) : first + width - half])
    return jnp.concatenate([own[rows], before[rows]] + far + [after[rows]], axis=0)


def values_kernel(place, arrived, *refs):
    later, weights = refs[:RING], refs[RING : RING + 5]
    outs = refs[-RING:]
    first_weights, later_weights = chunk_weights(0, *weights), chunk_weights(1, *weights)
    for k in (2, 1, 3, 0):
        y = lax.rem(place[0] + RING - k, RING)
        total = jnp.dot(arrived[y], first_weights, preferred_element_type=F32)
        total += jnp.dot(later[k][...], later_weights, preferred_element_type=F32)
        outs[k][...] = total.astype(outs[k].dtype)


def values_partial(place, arrived, later, weights, needed):
    tokens = arrived.shape[1]
    columns = weights[0].shape[1]
    shape = (tokens, columns)
    return pl.pallas_call(
        values_kernel,
        grid=(1,),
        out_shape=[pltpu.HBM(shape, F32 if k == 0 else BF16) for k in range(RING)],
        in_specs=[scalars(), pl.BlockSpec((RING, tokens, RING * CHUNKS[0][1]), lambda i: (0, 0, 0))]
        + [pl.BlockSpec(w.shape, lambda i: (0, 0)) for w in (*later, *weights)]
        + [pl.BlockSpec(memory_space=pl.ANY)] * len(needed),
        out_specs=[pl.BlockSpec(shape, lambda i: (0, 0))] * RING,
        compiler_params=params_of(),
        cost_estimate=COST,
        name="values_partial",
    )(place, arrived, *later, *weights, *needed)


def fragment_kernel(place, weights, anchor, moment, after, keep, send, state):
    del after
    height, width = keep.shape[1:]
    columns = pl.ds(pl.multiple_of(place[2] * width, width), width)
    core = lax.rem(place[3], 2)
    for pair in range(8):
        low = weights[2 * pair * height : (2 * pair + 1) * height, columns]
        high = weights[(2 * pair + 1) * height : (2 * pair + 2) * height, columns]
        keep[pair] = jnp.where(core == 0, low, high)
        send[pair] = jnp.where(core == 0, high, low)
    state[0] = anchor[:, columns]
    state[1] = moment[:, columns]


def fragment_columns(place, weights, anchor, moment, after):
    height, width = anchor.shape[0], weights.shape[1] // FRAG
    blocks = jax.ShapeDtypeStruct((8, height, width), F32)
    return pl.pallas_call(
        fragment_kernel,
        out_shape=[blocks, blocks, jax.ShapeDtypeStruct((2, height, width), F32)],
        in_specs=[scalars()] + whole(3) + [pl.BlockSpec(memory_space=pl.ANY)],
        out_specs=whole(3),
        compiler_params=params_of(),
        cost_estimate=COST,
        name="fragment_columns",
    )(place, weights, anchor, moment, after)


def forward_kernel(keep_left, keep_right, from_left, from_right, last_left, last_right):
    half = keep_left.shape[0]
    skip = from_left.shape[0] - 2 * half
    last_left[...] = (keep_left[...] + from_left[skip : skip + half].astype(F32)).astype(BF16)
    last_right[...] = (keep_right[...] + from_right[skip + half :].astype(F32)).astype(BF16)


def forward(keep_left, keep_right, from_left, from_right):
    return pl.pallas_call(
        forward_kernel,
        out_shape=[pltpu.HBM(keep_left.shape, BF16)] * 2,
        grid=(1,),
        in_specs=[pl.BlockSpec(a.shape, lambda i: (0, 0)) for a in (keep_left, keep_right, from_left, from_right)],
        out_specs=[pl.BlockSpec(keep_left.shape, lambda i: (0, 0))] * 2,
        compiler_params=params_of(),
        cost_estimate=COST,
        name="forward",
    )(keep_left, keep_right, from_left, from_right)


def outer_kernel(place, mine, other, theirs, anchor, moment, both, anchor_out, moment_out):
    height, width = anchor.shape[0], both.shape[2]
    zl = lax.rem(place[3] // 2, 2)
    columns = pl.ds(pl.multiple_of(place[2] * width, width), width)

    def update(index, old, old_moment):
        delta = old - (mine[index] + other[index]) / N_REP
        moment_new = OUTER_MOMENTUM * old_moment + delta
        new = old - OUTER_RATE * (delta + OUTER_MOMENTUM * moment_new)
        both[index] = new
        return new, moment_new

    new, moment_new = update(zl, anchor[:, columns], moment[:, columns])
    update(1 - zl, theirs[0], theirs[1])
    anchor_out[...] = anchor[...]
    moment_out[...] = moment[...]
    anchor_out[:, columns] = new
    moment_out[:, columns] = moment_new


def outer(place, mine, other, theirs, anchor, moment):
    shape = jax.ShapeDtypeStruct(anchor.shape, F32)
    return pl.pallas_call(
        outer_kernel,
        out_shape=[jax.ShapeDtypeStruct(mine.shape, F32), shape, shape],
        in_specs=[scalars()] + whole(5),
        out_specs=whole(3),
        compiler_params=params_of(),
        cost_estimate=COST,
        name="outer",
    )(place, mine, other, theirs, anchor, moment)


def values_sum_kernel(factor, own, one, two, three, out):
    total = own[...] + one[...].astype(F32) + two[...].astype(F32) + three[...].astype(F32)
    out[...] = (total * factor).astype(BF16)


def values_sum(factor, parts):
    shape = parts[0].shape
    return pl.pallas_call(
        functools.partial(values_sum_kernel, factor),
        grid=(1,),
        out_shape=jax.ShapeDtypeStruct(shape, BF16),
        in_specs=[pl.BlockSpec(shape, lambda i: (0, 0))] * RING,
        out_specs=pl.BlockSpec(shape, lambda i: (0, 0)),
        compiler_params=params_of(),
        cost_estimate=COST,
        name="values_sum",
    )(*parts)


def adam_kernel(place, rates, weights, first, second, *refs):
    own_0, left_0, right_0, own_1, left_1, right_1, last_left, last_right, near, far = refs[:10]
    out_weights, out_first, out_second = refs[10:]
    fragment, rep = place[2], place[3]
    x, core = rep // 4, lax.rem(rep, 2)
    rate, first_scale, second_scale, factor = rates[0], rates[1], rates[2], rates[3]
    part = pl.program_id(0)
    rows = weights.shape[0]
    skip = CHUNKS[0][1] // 2

    def step(total):
        gradient = total * factor
        first_new = FIRST_DECAY * first[...] + (1.0 - FIRST_DECAY) * gradient
        second_new = SECOND_DECAY * second[...] + (1.0 - SECOND_DECAY) * gradient * gradient
        out_first[...] = first_new
        out_second[...] = second_new
        update = (first_new * first_scale) / (jnp.sqrt(second_new * second_scale) + ADAM_EPSILON)
        out_weights[...] = weights[...] - rate * (update + WEIGHT_DECAY * weights[...])

    @pl.when(part == 0)
    def _():
        step(own_0[:rows] + right_0[:rows].astype(F32) + left_1[:rows].astype(F32))

    @pl.when(part == 1)
    def _():
        step(own_0[rows:] + left_0[rows:].astype(F32) + right_1[:rows].astype(F32))

    @pl.when(part == 2)
    def _():
        step(own_1[:rows] + right_1[skip : skip + rows].astype(F32) + last_left[...].astype(F32))

    @pl.when(part == 3)
    def _():
        step(own_1[rows:] + left_1[skip + rows :].astype(F32) + last_right[...].astype(F32))

    width = weights.shape[1] // FRAG
    height = near.shape[1]
    columns = pl.ds(pl.multiple_of(fragment * width, width), width)
    at = 2 * lax.rem(part // 2 + x // 2, 2) + 4 * lax.rem(part + x, 2)
    for block in range(4):
        index = at + block // 2
        base = jnp.where(core == block % 2, near[index], far[index])
        here = slice(block * height, (block + 1) * height)
        out_weights[here, columns] = base + (out_weights[here, columns] - weights[here, columns])


def adam(place, rates, weights, first, second, pieces, near, far):
    shape = jax.ShapeDtypeStruct(weights.shape, F32)
    rows = pl.BlockSpec((weights.shape[0] // 4, weights.shape[1]), lambda i: (i, 0))
    return pl.pallas_call(
        adam_kernel,
        grid=(4,),
        out_shape=[shape] * 3,
        in_specs=[scalars(), scalars(), rows, rows, rows]
        + [pl.BlockSpec(p.shape, lambda i: (0, 0)) for p in pieces]
        + [pl.BlockSpec(near.shape, lambda i: (0, 0, 0))] * 2,
        out_specs=[rows] * 3,
        compiler_params=params_of(),
        cost_estimate=COST,
        name="adam",
    )(place, rates, weights, first, second, *pieces, near, far)


def pick(array, index, axis):
    return lax.dynamic_index_in_dim(array, index, axis, keepdims=False)


def local(
    hidden,
    cotangent,
    norm_gain,
    params,
    adam_first,
    adam_second,
    outer_anchor,
    outer_momentum,
    fragment,
    inner_step,
):
    tokens = hidden[0]
    cot_local = cotangent[0]
    weights = params[0]
    factor = tokens.shape[1] ** (-0.5)
    shard = lax.axis_index("shard")
    rep = lax.axis_index("rep")
    place = jnp.stack([shard // RING, shard % RING, fragment, rep]).astype(jnp.int32)

    anchor_local, moment_local = outer_anchor[0, 0], outer_momentum[0, 0]
    gain = norm_gain.reshape(1, -1)

    packed, scale = first_pack(place, tokens, gain, cot_local)
    arrived = exchange_y(packed)

    weights_half = weights.astype(BF16)
    half = weights.shape[0] // 2
    before, after = shift_z(weights_half, 1), shift_z(weights_half, -1)
    far_top, far_bottom = shift_z(before[:half], 1), shift_z(after[half:], -1)
    ring_weights = [weights_half, before, far_top, far_bottom, after]

    keep, send, state = fragment_columns(place, weights, anchor_local, moment_local, scale)
    mine = jnp.concatenate([keep + swap_rep(send, 1), state])
    theirs = swap_rep(mine, 2)
    total = (mine[:8] + theirs[:8]).reshape(2, 2, 2, *keep.shape[1:])
    x_high, x_low = rep // 8, rep // 4 % 2
    total = pick(total, x_low, 1) + swap_rep(pick(total, 1 - x_low, 1), 4)
    other = swap_rep(pick(total, 1 - x_high, 0), 8)
    near, anchor_out, moment_out = outer(place, pick(total, x_high, 0), other, theirs[8:], anchor_local, moment_local)

    packed = later_pack(place, tokens, gain, scale, (near,))
    later = [packed[0]] + [shift_y(packed[k], k) for k in (1, 2, 3)]

    own_0, left, right, keep_left, keep_right = first_gradient(arrived, (before, after))
    left_0, right_0 = shift_z(left, -1), shift_z(right, 1)
    kept = (keep_left, keep_right, left_0, right_0)
    own_1, left, right, keep_left, keep_right = later_gradient(place, later, arrived, kept, ())
    near = jnp.concatenate([near, swap_rep(near, 8)])
    near = jnp.concatenate([near, swap_rep(near, 4)])
    far = swap_rep(near, 1)
    left_1, right_1 = shift_z(left, -1), shift_z(right, 1)
    last_left, last_right = forward(keep_left, keep_right, left_1, right_1)
    last_left, last_right = shift_z(last_left, -1), shift_z(last_right, 1)
    pieces = [own_0, left_0, right_0, own_1, left_1, right_1, last_left, last_right]

    partial = values_partial(place, arrived, later, ring_weights, (own_1,))
    value_rows = values_sum(factor, [partial[0]] + [shift_y(partial[k], -k) for k in (1, 2, 3)])

    clock = inner_step.astype(F32)
    rate = PEAK_RATE * 0.5 * (1.0 + jnp.cos(math.pi * clock / HORIZON_STEPS))
    first_scale = 1.0 / (1.0 - jnp.power(FIRST_DECAY, clock))
    second_scale = 1.0 / (1.0 - jnp.power(SECOND_DECAY, clock))
    rates = jnp.stack([rate, first_scale, second_scale, jnp.full((), factor, F32)])
    params_out, first_new, second_new = adam(
        place, rates, weights, adam_first[0], adam_second[0], pieces, near, far
    )
    return (
        value_rows[None],
        params_out[None],
        first_new[None],
        second_new[None],
        anchor_out[None, None],
        moment_out[None, None],
    )


def solution(mesh):
    in_specs = (
        P("rep", "shard", None),
        P("rep", "shard", None),
        P(),
        P("rep", "shard", None),
        P("rep", "shard", None),
        P("rep", "shard", None),
        P("shard", "rep", None, None),
        P("shard", "rep", None, None),
        P(),
        P(),
    )
    out_specs = (
        P("rep", "shard", None),
        P("rep", "shard", None),
        P("rep", "shard", None),
        P("rep", "shard", None),
        P("shard", "rep", None, None),
        P("shard", "rep", None, None),
    )
    return jax.shard_map(local, mesh=mesh, in_specs=in_specs, out_specs=out_specs, check_vma=False)
```

```python
import functools
import math

import jax
import jax.numpy as jnp
from jax import lax
from jax.experimental import pallas as pl
from jax.experimental.pallas import tpu as pltpu
from jax.sharding import PartitionSpec as P

FRAG = 4
RING = 4
N_REP = 16
CHUNKS = ((0, 256), (256, 256))

FIRST_DECAY = 0.9
SECOND_DECAY = 0.95
ADAM_EPSILON = 1e-08
PEAK_RATE = 0.125
WEIGHT_DECAY = 0.1
HORIZON_STEPS = 4096.0
OUTER_RATE = 0.7
OUTER_MOMENTUM = 0.9
NORM_EPSILON = 1e-05

COST = pl.CostEstimate(flops=1, bytes_accessed=1, transcendentals=0)
VMEM_LIMIT = 62 * 1024 * 1024
F32 = jnp.float32
BF16 = jnp.bfloat16


def exchange_y(array):
    groups = [[y * RING + z for y in range(RING)] for z in range(RING)]
    return lax.all_to_all(array, "shard", 0, 0, axis_index_groups=groups, tiled=True)


def shift_z(array, k):
    pairs = [(y * RING + z, y * RING + (z + k) % RING) for y in range(RING) for z in range(RING)]
    return lax.ppermute(array, "shard", pairs)


def swap_rep(array, bit):
    return lax.ppermute(array, "rep", [(r, r ^ bit) for r in range(16)])


def shift_y(array, k):
    pairs = [(y * RING + z, (y + k) % RING * RING + z) for y in range(RING) for z in range(RING)]
    return lax.ppermute(array, "shard", pairs)


def whole(n):
    return [pl.BlockSpec(memory_space=pltpu.VMEM)] * n


def scalars():
    return pl.BlockSpec(memory_space=pltpu.SMEM)


def params_of():
    return pltpu.CompilerParams(vmem_limit_bytes=VMEM_LIMIT)


def first_pack_kernel(place, hidden_ref, gain_ref, cot_ref, out, scale_ref):
    z = place[1]
    group = hidden_ref.shape[1] // RING
    block = group // RING
    first, width = CHUNKS[0]
    widened = hidden_ref[...].astype(F32)
    scale = lax.rsqrt(jnp.mean(widened * widened, axis=-1, keepdims=True) + NORM_EPSILON)
    scale_ref[...] = scale
    for y in range(RING):
        for kz in range(RING):
            start = y * group + lax.rem(z + RING - kz, RING) * block + first
            columns = pl.ds(pl.multiple_of(start, 128), width)
            normed = hidden_ref[:, columns].astype(F32) * scale * gain_ref[:, columns]
            out[y, :, kz * width : (kz + 1) * width] = normed.astype(BF16)
        out[y, :, RING * width :] = cot_ref[...]


def first_pack(place, hidden, gain, cot):
    tokens, features = hidden.shape
    columns = cot.shape[1]
    rows = 64
    total = RING * CHUNKS[0][1] + columns
    return pl.pallas_call(
        first_pack_kernel,
        out_shape=[pltpu.HBM((RING, tokens, total), BF16), pltpu.HBM((tokens, 1), F32)],
        grid_spec=pltpu.PrefetchScalarGridSpec(
            num_scalar_prefetch=1,
            grid=(tokens // rows,),
            in_specs=[
                pl.BlockSpec((rows, features), lambda i, place: (i, 0)),
                pl.BlockSpec((1, features), lambda i, place: (0, 0)),
                pl.BlockSpec((rows, columns), lambda i, place: (i, 0)),
            ],
            out_specs=[
                pl.BlockSpec((RING, rows, total), lambda i, place: (0, i, 0)),
                pl.BlockSpec((rows, 1), lambda i, place: (i, 0)),
            ],
        ),
        compiler_params=params_of(),
        cost_estimate=COST,
        name="first_pack",
    )(place, hidden, gain, cot)


def later_pack_kernel(place, *refs):
    hidden, gain, scale = refs[:RING], refs[RING : 2 * RING], refs[2 * RING]
    outs = refs[-RING:]
    for ky in range(RING):
        outs[ky][...] = (hidden[ky][...].astype(F32) * scale[...] * gain[ky][...]).astype(BF16)


def later_pack(place, hidden, gain, scale, after):
    tokens, features = hidden.shape
    first, width = CHUNKS[1]
    per_place = features // RING // RING // width

    def column(ky):
        def at(kz, place):
            whose = lax.rem(place[0] + ky, RING) * RING + lax.rem(place[1] + RING - kz, RING)
            return (0, whose * per_place + first // width)

        return at

    return pl.pallas_call(
        later_pack_kernel,
        out_shape=[pltpu.HBM((tokens, RING * width), BF16)] * RING,
        grid_spec=pltpu.PrefetchScalarGridSpec(
            num_scalar_prefetch=1,
            grid=(RING,),
            in_specs=[pl.BlockSpec((tokens, width), column(ky)) for ky in range(RING)]
            + [pl.BlockSpec((1, width), column(ky)) for ky in range(RING)]
            + [pl.BlockSpec((tokens, 1), lambda kz, place: (0, 0))]
            + [pl.BlockSpec(memory_space=pl.ANY)] * len(after),
            out_specs=[pl.BlockSpec((tokens, width), lambda kz, place: (0, kz))] * RING,
        ),
        compiler_params=params_of(),
        cost_estimate=COST,
        name="later_pack",
    )(place, *[hidden] * RING, *[gain] * RING, scale, *after)


def halves_kernel(before, after, *refs):
    top, bottom = refs[-2:]
    half = top.shape[0]
    top[...] = before[:half]
    bottom[...] = after[half:]


def halves(before, after, needed):
    rows, columns = before.shape
    whole_block = pl.BlockSpec((rows, columns), lambda i: (0, 0))
    half_block = pl.BlockSpec((rows // 2, columns), lambda i: (0, 0))
    return pl.pallas_call(
        halves_kernel,
        grid=(1,),
        out_shape=[pltpu.HBM((rows // 2, columns), BF16)] * 2,
        in_specs=[whole_block] * 2 + [pl.BlockSpec(memory_space=pl.ANY)] * len(needed),
        out_specs=[half_block] * 2,
        compiler_params=params_of(),
        cost_estimate=COST,
        name="halves",
    )(before, after, *needed)


def gradient_block(normed, cot, kz, height):
    rows = jnp.concatenate([n[:, kz * height : (kz + 1) * height] for n in normed], axis=0)
    return lax.dot_general(rows, cot, (((0,), (0,)), ((), ())), preferred_element_type=F32)


def gradient_blocks(normed, cot, own, left, right, keep_left, keep_right):
    height = own.shape[0]
    half = height // 2
    far = gradient_block(normed, cot, 2, height).astype(BF16)
    left[:half] = far[:half]
    right[half:] = far[half:]
    near = gradient_block(normed, cot, 1, height)
    keep_left[...] = near[:half]
    left[half:] = near[half:].astype(BF16)
    near = gradient_block(normed, cot, 3, height)
    keep_right[...] = near[half:]
    right[:half] = near[:half].astype(BF16)
    own[...] = gradient_block(normed, cot, 0, height)


def first_gradient_kernel(normed, cot, *refs):
    rows = [normed.at[y] for y in range(RING)]
    gradient_blocks(rows, jnp.concatenate([cot[y] for y in range(RING)], axis=0), *refs[-5:])


def first_gradient(arrived, after):
    tokens = arrived.shape[1]
    height = CHUNKS[0][1]
    columns = arrived.shape[2] - RING * height
    full, part = (height, columns), (height // 2, columns)
    shapes = [(full, F32), (full, BF16), (full, BF16), (part, F32), (part, F32)]
    cot_at = RING * height // columns
    return pl.pallas_call(
        first_gradient_kernel,
        grid=(1,),
        out_shape=[pltpu.HBM(*s) for s in shapes],
        in_specs=[
            pl.BlockSpec((RING, tokens, RING * height), lambda i: (0, 0, 0)),
            pl.BlockSpec((RING, tokens, columns), lambda i: (0, 0, cot_at)),
        ]
        + [pl.BlockSpec(memory_space=pl.ANY)] * len(after),
        out_specs=[pl.BlockSpec(s[0], lambda i: (0, 0)) for s in shapes],
        compiler_params=params_of(),
        cost_estimate=COST,
        name="first_gradient",
    )(arrived, arrived, *after)


def later_gradient_kernel(place, *refs):
    normed, cot = refs[:RING], refs[RING]
    own, left, right, next_left, next_right = refs[-5:]
    first = CHUNKS[0][1] // 2
    cot_all = jnp.concatenate([cot[lax.rem(place[0] + RING - k, RING)] for k in range(RING)], axis=0)
    for out in (left, right):
        out[:first] = jnp.zeros_like(out[:first])
    gradient_blocks(normed, cot_all, own, left.at[first:], right.at[first:], next_left, next_right)


def later_gradient(place, normed, arrived):
    tokens = arrived.shape[1]
    height = CHUNKS[1][1]
    columns = arrived.shape[2] - RING * CHUNKS[0][1]
    full, part = (height, columns), (height // 2, columns)
    sent = (height + CHUNKS[0][1] // 2, columns)
    shapes = [(full, F32), (sent, BF16), (sent, BF16), (part, F32), (part, F32)]
    cot_at = RING * CHUNKS[0][1] // columns
    return pl.pallas_call(
        later_gradient_kernel,
        grid=(1,),
        out_shape=[pltpu.HBM(*s) for s in shapes],
        in_specs=[scalars()]
        + [pl.BlockSpec((tokens, RING * height), lambda i: (0, 0))] * RING
        + [pl.BlockSpec((RING, tokens, columns), lambda i: (0, 0, cot_at))],
        out_specs=[pl.BlockSpec(s[0], lambda i: (0, 0)) for s in shapes],
        compiler_params=params_of(),
        cost_estimate=COST,
        name="later_gradient",
    )(place, *normed, arrived)


def join_kernel(keep_left, keep_right, from_left, from_right, *refs):
    left, right = refs[-2:]
    left[...] = (keep_left[...] + from_left[...].astype(F32)).astype(BF16)
    right[...] = (keep_right[...] + from_right[...].astype(F32)).astype(BF16)


def join(keep_left, keep_right, from_left, from_right, left, right):
    rows, columns = keep_left.shape
    top = pl.BlockSpec((rows, columns), lambda i: (0, 0))
    bottom = pl.BlockSpec((rows, columns), lambda i: (1, 0))
    anywhere = pl.BlockSpec(memory_space=pl.ANY)
    return pl.pallas_call(
        join_kernel,
        grid=(1,),
        out_shape=[pltpu.HBM(left.shape, BF16)] * 2,
        in_specs=[top, top, top, bottom, anywhere, anywhere],
        out_specs=[top, top],
        input_output_aliases={4: 0, 5: 1},
        compiler_params=params_of(),
        cost_estimate=COST,
        name="join",
    )(keep_left, keep_right, from_left, from_right, left, right)


def chunk_weights(chunk, own, before, far_top, far_bottom, after):
    first, width = CHUNKS[chunk]
    rows = slice(first, first + width)
    half = far_top.shape[0]
    far = []
    if first < half:
        far.append(far_top[first : min(first + width, half)])
    if first + width > half:
        far.append(far_bottom[max(first - half, 0) : first + width - half])
    return jnp.concatenate([own[rows], before[rows]] + far + [after[rows]], axis=0)


def values_kernel(place, arrived, *refs):
    later, weights = refs[:RING], refs[RING : RING + 5]
    outs = refs[-RING:]
    first_weights, later_weights = chunk_weights(0, *weights), chunk_weights(1, *weights)
    for k in (2, 1, 3, 0):
        y = lax.rem(place[0] + RING - k, RING)
        total = jnp.dot(arrived[y], first_weights, preferred_element_type=F32)
        total += jnp.dot(later[k][...], later_weights, preferred_element_type=F32)
        outs[k][...] = total.astype(outs[k].dtype)


def values_partial(place, arrived, later, weights, needed):
    tokens = arrived.shape[1]
    columns = weights[0].shape[1]
    shape = (tokens, columns)
    return pl.pallas_call(
        values_kernel,
        grid=(1,),
        out_shape=[pltpu.HBM(shape, F32 if k == 0 else BF16) for k in range(RING)],
        in_specs=[scalars(), pl.BlockSpec((RING, tokens, RING * CHUNKS[0][1]), lambda i: (0, 0, 0))]
        + [pl.BlockSpec(w.shape, lambda i: (0, 0)) for w in (*later, *weights)]
        + [pl.BlockSpec(memory_space=pl.ANY)] * len(needed),
        out_specs=[pl.BlockSpec(shape, lambda i: (0, 0))] * RING,
        compiler_params=params_of(),
        cost_estimate=COST,
        name="values_partial",
    )(place, arrived, *later, *weights, *needed)


def fragment_kernel(place, weights, anchor, moment, after, keep, send, state):
    del after
    height, width = keep.shape[1:]
    columns = pl.ds(pl.multiple_of(place[2] * width, width), width)
    core = lax.rem(place[3], 2)
    for pair in range(8):
        low = weights[2 * pair * height : (2 * pair + 1) * height, columns]
        high = weights[(2 * pair + 1) * height : (2 * pair + 2) * height, columns]
        keep[pair] = jnp.where(core == 0, low, high)
        send[pair] = jnp.where(core == 0, high, low)
    state[0] = anchor[:, columns]
    state[1] = moment[:, columns]


def fragment_columns(place, weights, anchor, moment, after):
    height, width = anchor.shape[0], weights.shape[1] // FRAG
    blocks = jax.ShapeDtypeStruct((8, height, width), F32)
    return pl.pallas_call(
        fragment_kernel,
        out_shape=[blocks, blocks, jax.ShapeDtypeStruct((2, height, width), F32)],
        in_specs=[scalars()] + whole(3) + [pl.BlockSpec(memory_space=pl.ANY)],
        out_specs=whole(3),
        compiler_params=params_of(),
        cost_estimate=COST,
        name="fragment_columns",
    )(place, weights, anchor, moment, after)


def forward_kernel(keep_left, keep_right, from_left, from_right, last_left, last_right):
    last_left[...] = (keep_left[...] + from_left[...].astype(F32)).astype(BF16)
    last_right[...] = (keep_right[...] + from_right[...].astype(F32)).astype(BF16)


def forward(keep_left, keep_right, from_left, from_right):
    rows, columns = keep_left.shape
    skip = CHUNKS[0][1] // 2 // rows
    first = pl.BlockSpec((rows, columns), lambda i: (0, 0))
    return pl.pallas_call(
        forward_kernel,
        grid=(1,),
        out_shape=[pltpu.HBM(keep_left.shape, BF16)] * 2,
        in_specs=[
            first,
            first,
            pl.BlockSpec((rows, columns), lambda i: (skip, 0)),
            pl.BlockSpec((rows, columns), lambda i: (skip + 1, 0)),
        ],
        out_specs=[first] * 2,
        compiler_params=params_of(),
        cost_estimate=COST,
        name="forward",
    )(keep_left, keep_right, from_left, from_right)


def outer_kernel(place, mine, other, theirs, anchor, moment, both, anchor_out, moment_out):
    height, width = anchor.shape[0], both.shape[2]
    zl = lax.rem(place[3] // 2, 2)
    columns = pl.ds(pl.multiple_of(place[2] * width, width), width)

    def update(index, old, old_moment):
        delta = old - (mine[index] + other[index]) / N_REP
        moment_new = OUTER_MOMENTUM * old_moment + delta
        new = old - OUTER_RATE * (delta + OUTER_MOMENTUM * moment_new)
        both[index] = new
        return new, moment_new

    new, moment_new = update(zl, anchor[:, columns], moment[:, columns])
    update(1 - zl, theirs[0], theirs[1])
    anchor_out[...] = anchor[...]
    moment_out[...] = moment[...]
    anchor_out[:, columns] = new
    moment_out[:, columns] = moment_new


def outer(place, mine, other, theirs, anchor, moment):
    shape = jax.ShapeDtypeStruct(anchor.shape, F32)
    return pl.pallas_call(
        outer_kernel,
        out_shape=[jax.ShapeDtypeStruct(mine.shape, F32), shape, shape],
        in_specs=[scalars()] + whole(5),
        out_specs=whole(3),
        compiler_params=params_of(),
        cost_estimate=COST,
        name="outer",
    )(place, mine, other, theirs, anchor, moment)


def values_sum_kernel(factor, own, one, two, three, out):
    total = own[...] + one[...].astype(F32) + two[...].astype(F32) + three[...].astype(F32)
    out[...] = (total * factor).astype(BF16)


def values_sum(factor, parts):
    shape = parts[0].shape
    return pl.pallas_call(
        functools.partial(values_sum_kernel, factor),
        grid=(1,),
        out_shape=jax.ShapeDtypeStruct(shape, BF16),
        in_specs=[pl.BlockSpec(shape, lambda i: (0, 0))] * RING,
        out_specs=pl.BlockSpec(shape, lambda i: (0, 0)),
        compiler_params=params_of(),
        cost_estimate=COST,
        name="values_sum",
    )(*parts)


def adam_kernel(chunk, place, rates, weights, first, second, own, left, right, last_left, last_right, near, far, *refs):
    out_weights, out_first, out_second = refs[-3:]
    fragment, rep = place[2], place[3]
    x, core = rep // 4, lax.rem(rep, 2)
    rate, first_scale, second_scale, factor = rates[0], rates[1], rates[2], rates[3]
    step_of = pl.program_id(0)
    part = 2 * chunk + step_of
    rows = weights.shape[0]
    skip = left.shape[0] - 2 * rows

    def step(total):
        gradient = total * factor
        first_new = FIRST_DECAY * first[...] + (1.0 - FIRST_DECAY) * gradient
        second_new = SECOND_DECAY * second[...] + (1.0 - SECOND_DECAY) * gradient * gradient
        out_first[...] = first_new
        out_second[...] = second_new
        update = (first_new * first_scale) / (jnp.sqrt(second_new * second_scale) + ADAM_EPSILON)
        out_weights[...] = weights[...] - rate * (update + WEIGHT_DECAY * weights[...])

    @pl.when(step_of == 0)
    def _():
        step(own[:rows] + right[skip : skip + rows].astype(F32) + last_left[:rows].astype(F32))

    @pl.when(step_of == 1)
    def _():
        step(own[rows:] + left[skip + rows :].astype(F32) + last_right[:rows].astype(F32))

    width = weights.shape[1] // FRAG
    height = near.shape[1]
    columns = pl.ds(pl.multiple_of(fragment * width, width), width)
    at = 2 * lax.rem(part // 2 + x // 2, 2) + 4 * lax.rem(part + x, 2)
    for block in range(4):
        index = at + block // 2
        base = jnp.where(core == block % 2, near[index], far[index])
        here = slice(block * height, (block + 1) * height)
        out_weights[here, columns] = base + (out_weights[here, columns] - weights[here, columns])


def adam(chunk, place, rates, weights, first, second, pieces, near, far, begun):
    shape = jax.ShapeDtypeStruct(weights.shape, F32)
    rows = pl.BlockSpec((weights.shape[0] // 4, weights.shape[1]), lambda i: (2 * chunk + i, 0))
    operands = (place, rates, weights, first, second, *pieces, near, far)
    return pl.pallas_call(
        functools.partial(adam_kernel, chunk),
        grid=(2,),
        out_shape=[shape] * 3,
        in_specs=[scalars(), scalars(), rows, rows, rows]
        + [pl.BlockSpec(p.shape, lambda i: (0, 0)) for p in pieces]
        + [pl.BlockSpec(near.shape, lambda i: (0, 0, 0))] * 2
        + [pl.BlockSpec(memory_space=pl.ANY)] * len(begun),
        out_specs=[rows] * 3,
        input_output_aliases={len(operands) + i: i for i in range(len(begun))},
        compiler_params=params_of(),
        cost_estimate=COST,
        name="adam",
    )(*operands, *begun)


def pick(array, index, axis):
    return lax.dynamic_index_in_dim(array, index, axis, keepdims=False)


def local(
    hidden,
    cotangent,
    norm_gain,
    params,
    adam_first,
    adam_second,
    outer_anchor,
    outer_momentum,
    fragment,
    inner_step,
):
    tokens = hidden[0]
    cot_local = cotangent[0]
    weights = params[0]
    factor = tokens.shape[1] ** (-0.5)
    shard = lax.axis_index("shard")
    rep = lax.axis_index("rep")
    place = jnp.stack([shard // RING, shard % RING, fragment, rep]).astype(jnp.int32)

    anchor_local, moment_local = outer_anchor[0, 0], outer_momentum[0, 0]
    gain = norm_gain.reshape(1, -1)

    packed, scale = first_pack(place, tokens, gain, cot_local)
    arrived = exchange_y(packed)

    weights_half = weights.astype(BF16)
    before, after = shift_z(weights_half, 1), shift_z(weights_half, -1)
    top, bottom = halves(before, after, ())
    far_top, far_bottom = shift_z(top, 1), shift_z(bottom, -1)
    ring_weights = [weights_half, before, far_top, far_bottom, after]

    keep, send, state = fragment_columns(place, weights, anchor_local, moment_local, scale)
    mine = jnp.concatenate([keep + swap_rep(send, 1), state])
    theirs = swap_rep(mine, 2)
    total = (mine[:8] + theirs[:8]).reshape(2, 2, 2, *keep.shape[1:])
    x_high, x_low = rep // 8, rep // 4 % 2
    total = pick(total, x_low, 1) + swap_rep(pick(total, 1 - x_low, 1), 4)
    other = swap_rep(pick(total, 1 - x_high, 0), 8)
    near, anchor_out, moment_out = outer(place, pick(total, x_high, 0), other, theirs[8:], anchor_local, moment_local)

    packed = later_pack(place, tokens, gain, scale, (near,))
    later = [packed[0]] + [shift_y(packed[k], k) for k in (1, 2, 3)]

    own_0, left, right, keep_left, keep_right = first_gradient(arrived, (before, after))
    left_0, right_0 = shift_z(left, -1), shift_z(right, 1)
    own_1, left, right, next_left, next_right = later_gradient(place, later, arrived)
    left, right = join(keep_left, keep_right, left_0, right_0, left, right)
    near = jnp.concatenate([near, swap_rep(near, 8)])
    near = jnp.concatenate([near, swap_rep(near, 4)])
    far = swap_rep(near, 1)
    left_1, right_1 = shift_z(left, -1), shift_z(right, 1)
    last_left, last_right = forward(next_left, next_right, left_1, right_1)
    last_left, last_right = shift_z(last_left, -1), shift_z(last_right, 1)
    pieces = ([own_0, left_0, right_0, left_1, right_1], [own_1, left_1, right_1, last_left, last_right])

    partial = values_partial(place, arrived, later, ring_weights, (own_1,))
    value_rows = values_sum(factor, [partial[0]] + [shift_y(partial[k], -k) for k in (1, 2, 3)])

    clock = inner_step.astype(F32)
    rate = PEAK_RATE * 0.5 * (1.0 + jnp.cos(math.pi * clock / HORIZON_STEPS))
    first_scale = 1.0 / (1.0 - jnp.power(FIRST_DECAY, clock))
    second_scale = 1.0 / (1.0 - jnp.power(SECOND_DECAY, clock))
    rates = jnp.stack([rate, first_scale, second_scale, jnp.full((), factor, F32)])
    begun = ()
    for chunk in range(len(CHUNKS)):
        begun = adam(
            chunk, place, rates, weights, adam_first[0], adam_second[0], pieces[chunk], near, far, begun
        )
    params_out, first_new, second_new = begun
    return (
        value_rows[None],
        params_out[None],
        first_new[None],
        second_new[None],
        anchor_out[None, None],
        moment_out[None, None],
    )


def solution(mesh):
    in_specs = (
        P("rep", "shard", None),
        P("rep", "shard", None),
        P(),
        P("rep", "shard", None),
        P("rep", "shard", None),
        P("rep", "shard", None),
        P("shard", "rep", None, None),
        P("shard", "rep", None, None),
        P(),
        P(),
    )
    out_specs = (
        P("rep", "shard", None),
        P("rep", "shard", None),
        P("rep", "shard", None),
        P("rep", "shard", None),
        P("shard", "rep", None, None),
        P("shard", "rep", None, None),
    )
    return jax.shard_map(local, mesh=mesh, in_specs=in_specs, out_specs=out_specs, check_vma=False)
```

```python
import functools
import math

import jax
import jax.numpy as jnp
from jax import lax
from jax.experimental import pallas as pl
from jax.experimental.pallas import tpu as pltpu
from jax.sharding import PartitionSpec as P

FRAG = 4
RING = 4
N_REP = 16
CHUNKS = ((0, 256), (256, 256))

FIRST_DECAY = 0.9
SECOND_DECAY = 0.95
ADAM_EPSILON = 1e-08
PEAK_RATE = 0.125
WEIGHT_DECAY = 0.1
HORIZON_STEPS = 4096.0
OUTER_RATE = 0.7
OUTER_MOMENTUM = 0.9
NORM_EPSILON = 1e-05

COST = pl.CostEstimate(flops=1, bytes_accessed=1, transcendentals=0)
VMEM_LIMIT = 62 * 1024 * 1024
F32 = jnp.float32
BF16 = jnp.bfloat16


def exchange_y(array):
    groups = [[y * RING + z for y in range(RING)] for z in range(RING)]
    return lax.all_to_all(array, "shard", 0, 0, axis_index_groups=groups, tiled=True)


def shift_z(array, k):
    pairs = [(y * RING + z, y * RING + (z + k) % RING) for y in range(RING) for z in range(RING)]
    return lax.ppermute(array, "shard", pairs)


def swap_rep(array, bit):
    return lax.ppermute(array, "rep", [(r, r ^ bit) for r in range(16)])


def shift_y(array, k):
    pairs = [(y * RING + z, (y + k) % RING * RING + z) for y in range(RING) for z in range(RING)]
    return lax.ppermute(array, "shard", pairs)


def whole(n):
    return [pl.BlockSpec(memory_space=pltpu.VMEM)] * n


def scalars():
    return pl.BlockSpec(memory_space=pltpu.SMEM)


def params_of():
    return pltpu.CompilerParams(vmem_limit_bytes=VMEM_LIMIT)


def first_pack_kernel(place, hidden_ref, gain_ref, cot_ref, out, scale_ref):
    z = place[1]
    group = hidden_ref.shape[1] // RING
    block = group // RING
    first, width = CHUNKS[0]
    widened = hidden_ref[...].astype(F32)
    scale = lax.rsqrt(jnp.mean(widened * widened, axis=-1, keepdims=True) + NORM_EPSILON)
    scale_ref[...] = scale
    for y in range(RING):
        for kz in range(RING):
            start = y * group + lax.rem(z + RING - kz, RING) * block + first
            columns = pl.ds(pl.multiple_of(start, 128), width)
            normed = hidden_ref[:, columns].astype(F32) * scale * gain_ref[:, columns]
            out[y, :, kz * width : (kz + 1) * width] = normed.astype(BF16)
        out[y, :, RING * width :] = cot_ref[...]


def first_pack(place, hidden, gain, cot):
    tokens, features = hidden.shape
    columns = cot.shape[1]
    rows = 128
    total = RING * CHUNKS[0][1] + columns
    return pl.pallas_call(
        first_pack_kernel,
        out_shape=[pltpu.HBM((RING, tokens, total), BF16), pltpu.HBM((tokens, 1), F32)],
        grid_spec=pltpu.PrefetchScalarGridSpec(
            num_scalar_prefetch=1,
            grid=(tokens // rows,),
            in_specs=[
                pl.BlockSpec((rows, features), lambda i, place: (i, 0)),
                pl.BlockSpec((1, features), lambda i, place: (0, 0)),
                pl.BlockSpec((rows, columns), lambda i, place: (i, 0)),
            ],
            out_specs=[
                pl.BlockSpec((RING, rows, total), lambda i, place: (0, i, 0)),
                pl.BlockSpec((rows, 1), lambda i, place: (i, 0)),
            ],
        ),
        compiler_params=params_of(),
        cost_estimate=COST,
        name="first_pack",
    )(place, hidden, gain, cot)


def later_pack_kernel(place, *refs):
    hidden, gain, scale = refs[:RING], refs[RING : 2 * RING], refs[2 * RING]
    outs = refs[-RING:]
    for ky in range(RING):
        outs[ky][...] = (hidden[ky][...].astype(F32) * scale[...] * gain[ky][...]).astype(BF16)


def later_pack(place, hidden, gain, scale, after):
    tokens, features = hidden.shape
    first, width = CHUNKS[1]
    per_place = features // RING // RING // width

    def column(ky):
        def at(kz, place):
            whose = lax.rem(place[0] + ky, RING) * RING + lax.rem(place[1] + RING - kz, RING)
            return (0, whose * per_place + first // width)

        return at

    return pl.pallas_call(
        later_pack_kernel,
        out_shape=[pltpu.HBM((tokens, RING * width), BF16)] * RING,
        grid_spec=pltpu.PrefetchScalarGridSpec(
            num_scalar_prefetch=1,
            grid=(RING,),
            in_specs=[pl.BlockSpec((tokens, width), column(ky)) for ky in range(RING)]
            + [pl.BlockSpec((1, width), column(ky)) for ky in range(RING)]
            + [pl.BlockSpec((tokens, 1), lambda kz, place: (0, 0))]
            + [pl.BlockSpec(memory_space=pl.ANY)] * len(after),
            out_specs=[pl.BlockSpec((tokens, width), lambda kz, place: (0, kz))] * RING,
        ),
        compiler_params=params_of(),
        cost_estimate=COST,
        name="later_pack",
    )(place, *[hidden] * RING, *[gain] * RING, scale, *after)


def gradient_block(normed, cot, kz, height):
    rows = jnp.concatenate([n[:, kz * height : (kz + 1) * height] for n in normed], axis=0)
    return lax.dot_general(rows, cot, (((0,), (0,)), ((), ())), preferred_element_type=F32)


def gradient_blocks(normed, cot, own, left, right, keep_left, keep_right):
    height = own.shape[0]
    half = height // 2
    far = gradient_block(normed, cot, 2, height).astype(BF16)
    left[:half] = far[:half]
    right[half:] = far[half:]
    near = gradient_block(normed, cot, 1, height)
    keep_left[...] = near[:half]
    left[half:] = near[half:].astype(BF16)
    near = gradient_block(normed, cot, 3, height)
    keep_right[...] = near[half:]
    right[:half] = near[:half].astype(BF16)
    own[...] = gradient_block(normed, cot, 0, height)


def first_gradient_kernel(normed, cot, before, after, own, left, right, keep_left, keep_right):
    rows = [normed.at[y] for y in range(RING)]
    height = own.shape[0]
    cot_all = jnp.concatenate([cot[y] for y in range(RING)], axis=0)
    gradient_blocks(rows, cot_all, own, left.at[:height], right.at[:height], keep_left, keep_right)
    left[height:] = after[...]
    right[height:] = before[...]


def first_gradient(arrived, before, after):
    tokens = arrived.shape[1]
    height = CHUNKS[0][1]
    columns = arrived.shape[2] - RING * height
    full, part = (height, columns), (height // 2, columns)
    rows = before.shape[0] // 2
    sent = (height + rows, columns)
    shapes = [(full, F32), (sent, BF16), (sent, BF16), (part, F32), (part, F32)]
    cot_at = RING * height // columns
    return pl.pallas_call(
        first_gradient_kernel,
        grid=(1,),
        out_shape=[pltpu.HBM(*s) for s in shapes],
        in_specs=[
            pl.BlockSpec((RING, tokens, RING * height), lambda i: (0, 0, 0)),
            pl.BlockSpec((RING, tokens, columns), lambda i: (0, 0, cot_at)),
            pl.BlockSpec((rows, columns), lambda i: (0, 0)),
            pl.BlockSpec((rows, columns), lambda i: (1, 0)),
        ],
        out_specs=[pl.BlockSpec(s[0], lambda i: (0, 0)) for s in shapes],
        compiler_params=params_of(),
        cost_estimate=COST,
        name="first_gradient",
    )(arrived, arrived, before, after)


def later_gradient_kernel(place, *refs):
    normed, cot = refs[:RING], refs[RING]
    own, left, right, next_left, next_right = refs[-5:]
    first = CHUNKS[0][1] // 2
    cot_all = jnp.concatenate([cot[lax.rem(place[0] + RING - k, RING)] for k in range(RING)], axis=0)
    for out in (left, right):
        out[:first] = jnp.zeros_like(out[:first])
    gradient_blocks(normed, cot_all, own, left.at[first:], right.at[first:], next_left, next_right)


def later_gradient(place, normed, arrived):
    tokens = arrived.shape[1]
    height = CHUNKS[1][1]
    columns = arrived.shape[2] - RING * CHUNKS[0][1]
    full, part = (height, columns), (height // 2, columns)
    sent = (height + CHUNKS[0][1] // 2, columns)
    shapes = [(full, F32), (sent, BF16), (sent, BF16), (part, F32), (part, F32)]
    cot_at = RING * CHUNKS[0][1] // columns
    return pl.pallas_call(
        later_gradient_kernel,
        grid=(1,),
        out_shape=[pltpu.HBM(*s) for s in shapes],
        in_specs=[scalars()]
        + [pl.BlockSpec((tokens, RING * height), lambda i: (0, 0))] * RING
        + [pl.BlockSpec((RING, tokens, columns), lambda i: (0, 0, cot_at))],
        out_specs=[pl.BlockSpec(s[0], lambda i: (0, 0)) for s in shapes],
        compiler_params=params_of(),
        cost_estimate=COST,
        name="later_gradient",
    )(place, *normed, arrived)


def join_kernel(keep_left, keep_right, from_left, from_right, *refs):
    left, right = refs[-2:]
    left[...] = (keep_left[...] + from_left[...].astype(F32)).astype(BF16)
    right[...] = (keep_right[...] + from_right[...].astype(F32)).astype(BF16)


def join(keep_left, keep_right, from_left, from_right, left, right):
    rows, columns = keep_left.shape
    top = pl.BlockSpec((rows, columns), lambda i: (0, 0))
    bottom = pl.BlockSpec((rows, columns), lambda i: (1, 0))
    anywhere = pl.BlockSpec(memory_space=pl.ANY)
    return pl.pallas_call(
        join_kernel,
        grid=(1,),
        out_shape=[pltpu.HBM(left.shape, BF16)] * 2,
        in_specs=[top, top, top, bottom, anywhere, anywhere],
        out_specs=[top, top],
        input_output_aliases={4: 0, 5: 1},
        compiler_params=params_of(),
        cost_estimate=COST,
        name="join",
    )(keep_left, keep_right, from_left, from_right, left, right)


def chunk_weights(chunk, own, before, far_top, far_bottom, after):
    first, width = CHUNKS[chunk]
    rows = slice(first, first + width)
    half = far_top.shape[0]
    far = []
    if first < half:
        far.append(far_top[first : min(first + width, half)])
    if first + width > half:
        far.append(far_bottom[max(first - half, 0) : first + width - half])
    return jnp.concatenate([own[rows], before[rows]] + far + [after[rows]], axis=0)


def values_kernel(place, arrived, *refs):
    later, weights = refs[:RING], refs[RING : RING + 5]
    outs = refs[-RING:]
    first_weights, later_weights = chunk_weights(0, *weights), chunk_weights(1, *weights)
    for k in (2, 1, 3, 0):
        y = lax.rem(place[0] + RING - k, RING)
        total = jnp.dot(arrived[y], first_weights, preferred_element_type=F32)
        total += jnp.dot(later[k][...], later_weights, preferred_element_type=F32)
        outs[k][...] = total.astype(outs[k].dtype)


def values_partial(place, arrived, later, weights, needed):
    tokens = arrived.shape[1]
    columns = weights[0].shape[1]
    shape = (tokens, columns)
    return pl.pallas_call(
        values_kernel,
        grid=(1,),
        out_shape=[pltpu.HBM(shape, F32 if k == 0 else BF16) for k in range(RING)],
        in_specs=[scalars(), pl.BlockSpec((RING, tokens, RING * CHUNKS[0][1]), lambda i: (0, 0, 0))]
        + [pl.BlockSpec(w.shape, lambda i: (0, 0)) for w in (*later, *weights[:2])]
        + [pl.BlockSpec((weights[0].shape[0] // 2, columns), lambda i: (1, 0))] * 2
        + [pl.BlockSpec(weights[4].shape, lambda i: (0, 0))]
        + [pl.BlockSpec(memory_space=pl.ANY)] * len(needed),
        out_specs=[pl.BlockSpec(shape, lambda i: (0, 0))] * RING,
        compiler_params=params_of(),
        cost_estimate=COST,
        name="values_partial",
    )(place, arrived, *later, *weights, *needed)


def fragment_kernel(place, weights, anchor, moment, after, keep, send, state):
    del after
    height, width = keep.shape[1:]
    columns = pl.ds(pl.multiple_of(place[2] * width, width), width)
    core = lax.rem(place[3], 2)
    for pair in range(8):
        low = weights[2 * pair * height : (2 * pair + 1) * height, columns]
        high = weights[(2 * pair + 1) * height : (2 * pair + 2) * height, columns]
        keep[pair] = jnp.where(core == 0, low, high)
        send[pair] = jnp.where(core == 0, high, low)
    state[0] = anchor[:, columns]
    state[1] = moment[:, columns]


def fragment_columns(place, weights, anchor, moment, after):
    height, width = anchor.shape[0], weights.shape[1] // FRAG
    blocks = jax.ShapeDtypeStruct((8, height, width), F32)
    return pl.pallas_call(
        fragment_kernel,
        out_shape=[blocks, blocks, jax.ShapeDtypeStruct((2, height, width), F32)],
        in_specs=[scalars()] + whole(3) + [pl.BlockSpec(memory_space=pl.ANY)],
        out_specs=whole(3),
        compiler_params=params_of(),
        cost_estimate=COST,
        name="fragment_columns",
    )(place, weights, anchor, moment, after)


def forward_kernel(keep_left, keep_right, from_left, from_right, last_left, last_right):
    last_left[...] = (keep_left[...] + from_left[...].astype(F32)).astype(BF16)
    last_right[...] = (keep_right[...] + from_right[...].astype(F32)).astype(BF16)


def forward(keep_left, keep_right, from_left, from_right):
    rows, columns = keep_left.shape
    skip = CHUNKS[0][1] // 2 // rows
    first = pl.BlockSpec((rows, columns), lambda i: (0, 0))
    return pl.pallas_call(
        forward_kernel,
        grid=(1,),
        out_shape=[pltpu.HBM(keep_left.shape, BF16)] * 2,
        in_specs=[
            first,
            first,
            pl.BlockSpec((rows, columns), lambda i: (skip, 0)),
            pl.BlockSpec((rows, columns), lambda i: (skip + 1, 0)),
        ],
        out_specs=[first] * 2,
        compiler_params=params_of(),
        cost_estimate=COST,
        name="forward",
    )(keep_left, keep_right, from_left, from_right)


def outer_kernel(place, mine, other, theirs, anchor, moment, both, anchor_out, moment_out):
    height, width = anchor.shape[0], both.shape[2]
    zl = lax.rem(place[3] // 2, 2)
    columns = pl.ds(pl.multiple_of(place[2] * width, width), width)

    def update(index, old, old_moment):
        delta = old - (mine[index] + other[index]) / N_REP
        moment_new = OUTER_MOMENTUM * old_moment + delta
        new = old - OUTER_RATE * (delta + OUTER_MOMENTUM * moment_new)
        both[index] = new
        return new, moment_new

    new, moment_new = update(zl, anchor[:, columns], moment[:, columns])
    update(1 - zl, theirs[0], theirs[1])
    anchor_out[...] = anchor[...]
    moment_out[...] = moment[...]
    anchor_out[:, columns] = new
    moment_out[:, columns] = moment_new


def outer(place, mine, other, theirs, anchor, moment):
    shape = jax.ShapeDtypeStruct(anchor.shape, F32)
    return pl.pallas_call(
        outer_kernel,
        out_shape=[jax.ShapeDtypeStruct(mine.shape, F32), shape, shape],
        in_specs=[scalars()] + whole(5),
        out_specs=whole(3),
        compiler_params=params_of(),
        cost_estimate=COST,
        name="outer",
    )(place, mine, other, theirs, anchor, moment)


def values_sum_kernel(factor, own, one, two, three, out):
    total = own[...] + one[...].astype(F32) + two[...].astype(F32) + three[...].astype(F32)
    out[...] = (total * factor).astype(BF16)


def values_sum(factor, parts):
    shape = parts[0].shape
    return pl.pallas_call(
        functools.partial(values_sum_kernel, factor),
        grid=(1,),
        out_shape=jax.ShapeDtypeStruct(shape, BF16),
        in_specs=[pl.BlockSpec(shape, lambda i: (0, 0))] * RING,
        out_specs=pl.BlockSpec(shape, lambda i: (0, 0)),
        compiler_params=params_of(),
        cost_estimate=COST,
        name="values_sum",
    )(*parts)


def adam_kernel(chunk, place, rates, weights, first, second, own, left, right, last_left, last_right, near, far, *refs):
    out_weights, out_first, out_second = refs[-3:]
    fragment, rep = place[2], place[3]
    x, core = rep // 4, lax.rem(rep, 2)
    rate, first_scale, second_scale, factor = rates[0], rates[1], rates[2], rates[3]
    rows = last_left.shape[0]
    skip = CHUNKS[0][1] // 2 if chunk else 0

    def step(half, total):
        here = slice(half * rows, (half + 1) * rows)
        gradient = total * factor
        first_new = FIRST_DECAY * first[here] + (1.0 - FIRST_DECAY) * gradient
        second_new = SECOND_DECAY * second[here] + (1.0 - SECOND_DECAY) * gradient * gradient
        out_first[here] = first_new
        out_second[here] = second_new
        update = (first_new * first_scale) / (jnp.sqrt(second_new * second_scale) + ADAM_EPSILON)
        out_weights[here] = weights[here] - rate * (update + WEIGHT_DECAY * weights[here])

    step(0, own[:rows] + right[skip : skip + rows].astype(F32) + last_left[...].astype(F32))
    step(1, own[rows:] + left[skip + rows :].astype(F32) + last_right[...].astype(F32))

    width = weights.shape[1] // FRAG
    height = near.shape[1]
    columns = pl.ds(pl.multiple_of(fragment * width, width), width)
    for block in range(weights.shape[0] // height):
        part = 2 * chunk + block // 4
        index = 2 * lax.rem(part // 2 + x // 2, 2) + 4 * lax.rem(part + x, 2) + block % 4 // 2
        base = jnp.where(core == block % 2, near[index], far[index])
        lines = slice(block * height, (block + 1) * height)
        out_weights[lines, columns] = base + (out_weights[lines, columns] - weights[lines, columns])


def adam(chunk, place, rates, weights, first, second, pieces, near, far, begun):
    shape = jax.ShapeDtypeStruct(weights.shape, F32)
    rows = pl.BlockSpec((CHUNKS[chunk][1], weights.shape[1]), lambda i: (chunk, 0))
    half = CHUNKS[chunk][1] // 2
    skip = CHUNKS[0][1] // 2 if chunk else 0
    used = (2 * half, skip + 2 * half, skip + 2 * half, half, half)
    operands = (place, rates, weights, first, second, *pieces, near, far)
    return pl.pallas_call(
        functools.partial(adam_kernel, chunk),
        grid=(1,),
        out_shape=[shape] * 3,
        in_specs=[scalars(), scalars(), rows, rows, rows]
        + [pl.BlockSpec((n, p.shape[1]), lambda i: (0, 0)) for n, p in zip(used, pieces)]
        + [pl.BlockSpec(near.shape, lambda i: (0, 0, 0))] * 2
        + [pl.BlockSpec(memory_space=pl.ANY)] * len(begun),
        out_specs=[rows] * 3,
        input_output_aliases={len(operands) + i: i for i in range(len(begun))},
        compiler_params=params_of(),
        cost_estimate=COST,
        name="adam",
    )(*operands, *begun)


def pick(array, index, axis):
    return lax.dynamic_index_in_dim(array, index, axis, keepdims=False)


def local(
    hidden,
    cotangent,
    norm_gain,
    params,
    adam_first,
    adam_second,
    outer_anchor,
    outer_momentum,
    fragment,
    inner_step,
):
    tokens = hidden[0]
    cot_local = cotangent[0]
    weights = params[0]
    factor = tokens.shape[1] ** (-0.5)
    shard = lax.axis_index("shard")
    rep = lax.axis_index("rep")
    place = jnp.stack([shard // RING, shard % RING, fragment, rep]).astype(jnp.int32)

    anchor_local, moment_local = outer_anchor[0, 0], outer_momentum[0, 0]
    gain = norm_gain.reshape(1, -1)

    packed, scale = first_pack(place, tokens, gain, cot_local)
    arrived = exchange_y(packed)

    weights_half = weights.astype(BF16)
    before, after = shift_z(weights_half, 1), shift_z(weights_half, -1)

    keep, send, state = fragment_columns(place, weights, anchor_local, moment_local, scale)
    mine = jnp.concatenate([keep + swap_rep(send, 1), state])
    theirs = swap_rep(mine, 2)
    total = (mine[:8] + theirs[:8]).reshape(2, 2, 2, *keep.shape[1:])
    x_high, x_low = rep // 8, rep // 4 % 2
    total = pick(total, x_low, 1) + swap_rep(pick(total, 1 - x_low, 1), 4)
    other = swap_rep(pick(total, 1 - x_high, 0), 8)
    near, anchor_out, moment_out = outer(place, pick(total, x_high, 0), other, theirs[8:], anchor_local, moment_local)

    packed = later_pack(place, tokens, gain, scale, (near,))
    later = [packed[0]] + [shift_y(packed[k], k) for k in (1, 2, 3)]

    own_0, left, right, keep_left, keep_right = first_gradient(arrived, before, after)
    left_0, right_0 = shift_z(left, -1), shift_z(right, 1)
    ring_weights = [weights_half, before, right_0, left_0, after]
    own_1, left, right, next_left, next_right = later_gradient(place, later, arrived)
    left, right = join(keep_left, keep_right, left_0, right_0, left, right)
    near = jnp.concatenate([near, swap_rep(near, 8)])
    near = jnp.concatenate([near, swap_rep(near, 4)])
    far = swap_rep(near, 1)
    left_1, right_1 = shift_z(left, -1), shift_z(right, 1)
    last_left, last_right = forward(next_left, next_right, left_1, right_1)
    last_left, last_right = shift_z(last_left, -1), shift_z(last_right, 1)
    pieces = ([own_0, left_0, right_0, left_1, right_1], [own_1, left_1, right_1, last_left, last_right])

    partial = values_partial(place, arrived, later, ring_weights, (own_1,))
    value_rows = values_sum(factor, [partial[0]] + [shift_y(partial[k], -k) for k in (1, 2, 3)])

    clock = inner_step.astype(F32)
    rate = PEAK_RATE * 0.5 * (1.0 + jnp.cos(math.pi * clock / HORIZON_STEPS))
    first_scale = 1.0 / (1.0 - jnp.power(FIRST_DECAY, clock))
    second_scale = 1.0 / (1.0 - jnp.power(SECOND_DECAY, clock))
    rates = jnp.stack([rate, first_scale, second_scale, jnp.full((), factor, F32)])
    begun = ()
    for chunk in range(len(CHUNKS)):
        begun = adam(
            chunk, place, rates, weights, adam_first[0], adam_second[0], pieces[chunk], near, far, begun
        )
    params_out, first_new, second_new = begun
    return (
        value_rows[None],
        params_out[None],
        first_new[None],
        second_new[None],
        anchor_out[None, None],
        moment_out[None, None],
    )


def solution(mesh):
    in_specs = (
        P("rep", "shard", None),
        P("rep", "shard", None),
        P(),
        P("rep", "shard", None),
        P("rep", "shard", None),
        P("rep", "shard", None),
        P("shard", "rep", None, None),
        P("shard", "rep", None, None),
        P(),
        P(),
    )
    out_specs = (
        P("rep", "shard", None),
        P("rep", "shard", None),
        P("rep", "shard", None),
        P("rep", "shard", None),
        P("shard", "rep", None, None),
        P("shard", "rep", None, None),
    )
    return jax.shard_map(local, mesh=mesh, in_specs=in_specs, out_specs=out_specs, check_vma=False)
```

```python
import functools
import math

import jax
import jax.numpy as jnp
from jax import lax
from jax.experimental import pallas as pl
from jax.experimental.pallas import tpu as pltpu
from jax.sharding import PartitionSpec as P

FRAG = 4
RING = 4
N_REP = 16
CHUNKS = ((0, 256), (256, 256))

FIRST_DECAY = 0.9
SECOND_DECAY = 0.95
ADAM_EPSILON = 1e-08
PEAK_RATE = 0.125
WEIGHT_DECAY = 0.1
HORIZON_STEPS = 4096.0
OUTER_RATE = 0.7
OUTER_MOMENTUM = 0.9
NORM_EPSILON = 1e-05

COST = pl.CostEstimate(flops=1, bytes_accessed=1, transcendentals=0)
VMEM_LIMIT = 62 * 1024 * 1024
F32 = jnp.float32
BF16 = jnp.bfloat16


def exchange_y(array):
    groups = [[y * RING + z for y in range(RING)] for z in range(RING)]
    return lax.all_to_all(array, "shard", 0, 0, axis_index_groups=groups, tiled=True)


def shift_z(array, k):
    pairs = [(y * RING + z, y * RING + (z + k) % RING) for y in range(RING) for z in range(RING)]
    return lax.ppermute(array, "shard", pairs)


def swap_rep(array, bit):
    return lax.ppermute(array, "rep", [(r, r ^ bit) for r in range(16)])


def shift_y(array, k):
    pairs = [(y * RING + z, (y + k) % RING * RING + z) for y in range(RING) for z in range(RING)]
    return lax.ppermute(array, "shard", pairs)


def whole(n):
    return [pl.BlockSpec(memory_space=pltpu.VMEM)] * n


def scalars():
    return pl.BlockSpec(memory_space=pltpu.SMEM)


def params_of():
    return pltpu.CompilerParams(vmem_limit_bytes=VMEM_LIMIT)


def first_pack_kernel(place, hidden_ref, gain_ref, cot_ref, out, scale_ref):
    z = place[1]
    group = hidden_ref.shape[1] // RING
    block = group // RING
    first, width = CHUNKS[0]
    widened = hidden_ref[...].astype(F32)
    scale = lax.rsqrt(jnp.mean(widened * widened, axis=-1, keepdims=True) + NORM_EPSILON)
    scale_ref[...] = scale
    for y in range(RING):
        for kz in range(RING):
            start = y * group + lax.rem(z + RING - kz, RING) * block + first
            columns = pl.ds(pl.multiple_of(start, 128), width)
            normed = hidden_ref[:, columns].astype(F32) * scale * gain_ref[:, columns]
            out[y, :, kz * width : (kz + 1) * width] = normed.astype(BF16)
        out[y, :, RING * width :] = cot_ref[...]


def first_pack(place, hidden, gain, cot):
    tokens, features = hidden.shape
    columns = cot.shape[1]
    rows = 128
    total = RING * CHUNKS[0][1] + columns
    return pl.pallas_call(
        first_pack_kernel,
        out_shape=[pltpu.HBM((RING, tokens, total), BF16), pltpu.HBM((tokens, 1), F32)],
        grid_spec=pltpu.PrefetchScalarGridSpec(
            num_scalar_prefetch=1,
            grid=(tokens // rows,),
            in_specs=[
                pl.BlockSpec((rows, features), lambda i, place: (i, 0)),
                pl.BlockSpec((1, features), lambda i, place: (0, 0)),
                pl.BlockSpec((rows, columns), lambda i, place: (i, 0)),
            ],
            out_specs=[
                pl.BlockSpec((RING, rows, total), lambda i, place: (0, i, 0)),
                pl.BlockSpec((rows, 1), lambda i, place: (i, 0)),
            ],
        ),
        compiler_params=params_of(),
        cost_estimate=COST,
        name="first_pack",
    )(place, hidden, gain, cot)


def later_pack_kernel(place, *refs):
    hidden, gain, scale = refs[:RING], refs[RING : 2 * RING], refs[2 * RING]
    outs = refs[-RING:]
    for ky in range(RING):
        outs[ky][...] = (hidden[ky][...].astype(F32) * scale[...] * gain[ky][...]).astype(BF16)


def later_pack(place, hidden, gain, scale, after):
    tokens, features = hidden.shape
    first, width = CHUNKS[1]
    per_place = features // RING // RING // width

    def column(ky):
        def at(kz, place):
            whose = lax.rem(place[0] + ky, RING) * RING + lax.rem(place[1] + RING - kz, RING)
            return (0, whose * per_place + first // width)

        return at

    return pl.pallas_call(
        later_pack_kernel,
        out_shape=[pltpu.HBM((tokens, RING * width), BF16)] * RING,
        grid_spec=pltpu.PrefetchScalarGridSpec(
            num_scalar_prefetch=1,
            grid=(RING,),
            in_specs=[pl.BlockSpec((tokens, width), column(ky)) for ky in range(RING)]
            + [pl.BlockSpec((1, width), column(ky)) for ky in range(RING)]
            + [pl.BlockSpec((tokens, 1), lambda kz, place: (0, 0))]
            + [pl.BlockSpec(memory_space=pl.ANY)] * len(after),
            out_specs=[pl.BlockSpec((tokens, width), lambda kz, place: (0, kz))] * RING,
        ),
        compiler_params=params_of(),
        cost_estimate=COST,
        name="later_pack",
    )(place, *[hidden] * RING, *[gain] * RING, scale, *after)


def gradient_block(normed, cot, kz, height):
    rows = jnp.concatenate([n[:, kz * height : (kz + 1) * height] for n in normed], axis=0)
    return lax.dot_general(rows, cot, (((0,), (0,)), ((), ())), preferred_element_type=F32)


def gradient_blocks(normed, cot, own, left, right, keep_left, keep_right):
    height = own.shape[0]
    half = height // 2
    far = gradient_block(normed, cot, 2, height).astype(BF16)
    left[:half] = far[:half]
    right[half:] = far[half:]
    near = gradient_block(normed, cot, 1, height)
    keep_left[...] = near[:half]
    left[half:] = near[half:].astype(BF16)
    near = gradient_block(normed, cot, 3, height)
    keep_right[...] = near[half:]
    right[:half] = near[:half].astype(BF16)
    own[...] = gradient_block(normed, cot, 0, height)


def first_gradient_kernel(normed, cot, before, after, own, left, right, keep_left, keep_right):
    rows = [normed.at[y] for y in range(RING)]
    height = own.shape[0]
    cot_all = jnp.concatenate([cot[y] for y in range(RING)], axis=0)
    gradient_blocks(rows, cot_all, own, left.at[:height], right.at[:height], keep_left, keep_right)
    left[height:] = after[...]
    right[height:] = before[...]


def first_gradient(arrived, before, after):
    tokens = arrived.shape[1]
    height = CHUNKS[0][1]
    columns = arrived.shape[2] - RING * height
    full, part = (height, columns), (height // 2, columns)
    rows = before.shape[0] // 2
    sent = (height + rows, columns)
    shapes = [(full, F32), (sent, BF16), (sent, BF16), (part, F32), (part, F32)]
    cot_at = RING * height // columns
    return pl.pallas_call(
        first_gradient_kernel,
        grid=(1,),
        out_shape=[pltpu.HBM(*s) for s in shapes],
        in_specs=[
            pl.BlockSpec((RING, tokens, RING * height), lambda i: (0, 0, 0)),
            pl.BlockSpec((RING, tokens, columns), lambda i: (0, 0, cot_at)),
            pl.BlockSpec((rows, columns), lambda i: (0, 0)),
            pl.BlockSpec((rows, columns), lambda i: (1, 0)),
        ],
        out_specs=[pl.BlockSpec(s[0], lambda i: (0, 0)) for s in shapes],
        compiler_params=params_of(),
        cost_estimate=COST,
        name="first_gradient",
    )(arrived, arrived, before, after)


def later_gradient_kernel(place, *refs):
    normed, cot = refs[:RING], refs[RING]
    own, left, right, next_left, next_right = refs[-5:]
    first = CHUNKS[0][1] // 2
    cot_all = jnp.concatenate([cot[lax.rem(place[0] + RING - k, RING)] for k in range(RING)], axis=0)
    for out in (left, right):
        out[:first] = jnp.zeros_like(out[:first])
    gradient_blocks(normed, cot_all, own, left.at[first:], right.at[first:], next_left, next_right)


def later_gradient(place, normed, arrived):
    tokens = arrived.shape[1]
    height = CHUNKS[1][1]
    columns = arrived.shape[2] - RING * CHUNKS[0][1]
    full, part = (height, columns), (height // 2, columns)
    sent = (height + CHUNKS[0][1] // 2, columns)
    shapes = [(full, F32), (sent, BF16), (sent, BF16), (part, F32), (part, F32)]
    cot_at = RING * CHUNKS[0][1] // columns
    return pl.pallas_call(
        later_gradient_kernel,
        grid=(1,),
        out_shape=[pltpu.HBM(*s) for s in shapes],
        in_specs=[scalars()]
        + [pl.BlockSpec((tokens, RING * height), lambda i: (0, 0))] * RING
        + [pl.BlockSpec((RING, tokens, columns), lambda i: (0, 0, cot_at))],
        out_specs=[pl.BlockSpec(s[0], lambda i: (0, 0)) for s in shapes],
        compiler_params=params_of(),
        cost_estimate=COST,
        name="later_gradient",
    )(place, *normed, arrived)


def join_kernel(keep_left, keep_right, from_left, from_right, *refs):
    left, right = refs[-2:]
    left[...] = (keep_left[...] + from_left[...].astype(F32)).astype(BF16)
    right[...] = (keep_right[...] + from_right[...].astype(F32)).astype(BF16)


def join(keep_left, keep_right, from_left, from_right, left, right):
    rows, columns = keep_left.shape
    top = pl.BlockSpec((rows, columns), lambda i: (0, 0))
    bottom = pl.BlockSpec((rows, columns), lambda i: (1, 0))
    anywhere = pl.BlockSpec(memory_space=pl.ANY)
    return pl.pallas_call(
        join_kernel,
        grid=(1,),
        out_shape=[pltpu.HBM(left.shape, BF16)] * 2,
        in_specs=[top, top, top, bottom, anywhere, anywhere],
        out_specs=[top, top],
        input_output_aliases={4: 0, 5: 1},
        compiler_params=params_of(),
        cost_estimate=COST,
        name="join",
    )(keep_left, keep_right, from_left, from_right, left, right)


def near_values_kernel(place, arrived, *refs):
    later, (own, before, after) = refs[:RING], refs[RING : RING + 3]
    out = refs[-1]
    (_, early), (start, late) = CHUNKS
    for k in range(RING):
        y = lax.rem(place[0] + RING - k, RING)
        total = jnp.zeros(out.shape[1:], F32)
        for kz, weights in ((0, own), (1, before), (3, after)):
            rows = arrived[y, :, kz * early : (kz + 1) * early]
            total += jnp.dot(rows, weights[:start], preferred_element_type=F32)
            rows = later[k][:, kz * late : (kz + 1) * late]
            total += jnp.dot(rows, weights[start:], preferred_element_type=F32)
        out[k] = total


def near_values(place, arrived, later, weights, needed):
    tokens, columns = arrived.shape[1], weights[0].shape[1]
    shape = (RING, tokens, columns)
    return pl.pallas_call(
        near_values_kernel,
        grid=(1,),
        out_shape=pltpu.HBM(shape, F32),
        in_specs=[scalars(), pl.BlockSpec((RING, tokens, RING * CHUNKS[0][1]), lambda i: (0, 0, 0))]
        + [pl.BlockSpec(w.shape, lambda i: (0, 0)) for w in (*later, *weights)]
        + [pl.BlockSpec(memory_space=pl.ANY)] * len(needed),
        out_specs=pl.BlockSpec(shape, lambda i: (0, 0, 0)),
        compiler_params=params_of(),
        cost_estimate=COST,
        name="near_values",
    )(place, arrived, *later, *weights, *needed)


def far_values_kernel(place, total, arrived, *refs):
    later, (top, bottom) = refs[:RING], refs[RING : RING + 2]
    outs = refs[-RING:]
    for k in (2, 1, 3, 0):
        y = lax.rem(place[0] + RING - k, RING)
        share = total[k] + jnp.dot(arrived[y], top[...], preferred_element_type=F32)
        share += jnp.dot(later[k][...], bottom[...], preferred_element_type=F32)
        outs[k][...] = share.astype(outs[k].dtype)


def far_values(place, total, arrived, later, top, bottom):
    tokens, columns = total.shape[1:]
    (_, early), (_, late) = CHUNKS
    shape = (tokens, columns)
    return pl.pallas_call(
        far_values_kernel,
        grid=(1,),
        out_shape=[pltpu.HBM(shape, F32 if k == 0 else BF16) for k in range(RING)],
        in_specs=[
            scalars(),
            pl.BlockSpec(total.shape, lambda i: (0, 0, 0)),
            pl.BlockSpec((RING, tokens, early), lambda i: (0, 0, 2)),
        ]
        + [pl.BlockSpec((tokens, late), lambda i: (0, 2))] * RING
        + [pl.BlockSpec((early, columns), lambda i: (1, 0)), pl.BlockSpec((late, columns), lambda i: (1, 0))],
        out_specs=[pl.BlockSpec(shape, lambda i: (0, 0))] * RING,
        compiler_params=params_of(),
        cost_estimate=COST,
        name="far_values",
    )(place, total, arrived, *later, top, bottom)


def fragment_kernel(place, weights, anchor, moment, after, keep, send, state):
    del after
    height, width = keep.shape[1:]
    columns = pl.ds(pl.multiple_of(place[2] * width, width), width)
    core = lax.rem(place[3], 2)
    for pair in range(8):
        low = weights[2 * pair * height : (2 * pair + 1) * height, columns]
        high = weights[(2 * pair + 1) * height : (2 * pair + 2) * height, columns]
        keep[pair] = jnp.where(core == 0, low, high)
        send[pair] = jnp.where(core == 0, high, low)
    state[0] = anchor[:, columns]
    state[1] = moment[:, columns]


def fragment_columns(place, weights, anchor, moment, after):
    height, width = anchor.shape[0], weights.shape[1] // FRAG
    blocks = jax.ShapeDtypeStruct((8, height, width), F32)
    return pl.pallas_call(
        fragment_kernel,
        out_shape=[blocks, blocks, jax.ShapeDtypeStruct((2, height, width), F32)],
        in_specs=[scalars()] + whole(3) + [pl.BlockSpec(memory_space=pl.ANY)],
        out_specs=whole(3),
        compiler_params=params_of(),
        cost_estimate=COST,
        name="fragment_columns",
    )(place, weights, anchor, moment, after)


def forward_kernel(keep_left, keep_right, from_left, from_right, last_left, last_right):
    last_left[...] = (keep_left[...] + from_left[...].astype(F32)).astype(BF16)
    last_right[...] = (keep_right[...] + from_right[...].astype(F32)).astype(BF16)


def forward(keep_left, keep_right, from_left, from_right):
    rows, columns = keep_left.shape
    skip = CHUNKS[0][1] // 2 // rows
    first = pl.BlockSpec((rows, columns), lambda i: (0, 0))
    return pl.pallas_call(
        forward_kernel,
        grid=(1,),
        out_shape=[pltpu.HBM(keep_left.shape, BF16)] * 2,
        in_specs=[
            first,
            first,
            pl.BlockSpec((rows, columns), lambda i: (skip, 0)),
            pl.BlockSpec((rows, columns), lambda i: (skip + 1, 0)),
        ],
        out_specs=[first] * 2,
        compiler_params=params_of(),
        cost_estimate=COST,
        name="forward",
    )(keep_left, keep_right, from_left, from_right)


def outer_kernel(place, mine, other, theirs, anchor, moment, both, anchor_out, moment_out):
    height, width = anchor.shape[0], both.shape[2]
    zl = lax.rem(place[3] // 2, 2)
    columns = pl.ds(pl.multiple_of(place[2] * width, width), width)

    def update(index, old, old_moment):
        delta = old - (mine[index] + other[index]) / N_REP
        moment_new = OUTER_MOMENTUM * old_moment + delta
        new = old - OUTER_RATE * (delta + OUTER_MOMENTUM * moment_new)
        both[index] = new
        return new, moment_new

    new, moment_new = update(zl, anchor[:, columns], moment[:, columns])
    update(1 - zl, theirs[0], theirs[1])
    anchor_out[...] = anchor[...]
    moment_out[...] = moment[...]
    anchor_out[:, columns] = new
    moment_out[:, columns] = moment_new


def outer(place, mine, other, theirs, anchor, moment):
    shape = jax.ShapeDtypeStruct(anchor.shape, F32)
    return pl.pallas_call(
        outer_kernel,
        out_shape=[jax.ShapeDtypeStruct(mine.shape, F32), shape, shape],
        in_specs=[scalars()] + whole(5),
        out_specs=whole(3),
        compiler_params=params_of(),
        cost_estimate=COST,
        name="outer",
    )(place, mine, other, theirs, anchor, moment)


def values_sum_kernel(factor, own, one, two, three, out):
    total = own[...] + one[...].astype(F32) + two[...].astype(F32) + three[...].astype(F32)
    out[...] = (total * factor).astype(BF16)


def values_sum(factor, parts):
    shape = parts[0].shape
    return pl.pallas_call(
        functools.partial(values_sum_kernel, factor),
        grid=(1,),
        out_shape=jax.ShapeDtypeStruct(shape, BF16),
        in_specs=[pl.BlockSpec(shape, lambda i: (0, 0))] * RING,
        out_specs=pl.BlockSpec(shape, lambda i: (0, 0)),
        compiler_params=params_of(),
        cost_estimate=COST,
        name="values_sum",
    )(*parts)


def adam_kernel(chunk, place, rates, weights, first, second, own, left, right, last_left, last_right, near, far, *refs):
    out_weights, out_first, out_second = refs[-3:]
    fragment, rep = place[2], place[3]
    x, core = rep // 4, lax.rem(rep, 2)
    rate, first_scale, second_scale, factor = rates[0], rates[1], rates[2], rates[3]
    rows = last_left.shape[0]
    skip = CHUNKS[0][1] // 2 if chunk else 0

    def step(half, total):
        here = slice(half * rows, (half + 1) * rows)
        gradient = total * factor
        first_new = FIRST_DECAY * first[here] + (1.0 - FIRST_DECAY) * gradient
        second_new = SECOND_DECAY * second[here] + (1.0 - SECOND_DECAY) * gradient * gradient
        out_first[here] = first_new
        out_second[here] = second_new
        update = (first_new * first_scale) / (jnp.sqrt(second_new * second_scale) + ADAM_EPSILON)
        out_weights[here] = weights[here] - rate * (update + WEIGHT_DECAY * weights[here])

    step(0, own[:rows] + right[skip : skip + rows].astype(F32) + last_left[...].astype(F32))
    step(1, own[rows:] + left[skip + rows :].astype(F32) + last_right[...].astype(F32))

    width = weights.shape[1] // FRAG
    height = near.shape[1]
    columns = pl.ds(pl.multiple_of(fragment * width, width), width)
    for block in range(weights.shape[0] // height):
        part = 2 * chunk + block // 4
        index = 2 * lax.rem(part // 2 + x // 2, 2) + 4 * lax.rem(part + x, 2) + block % 4 // 2
        base = jnp.where(core == block % 2, near[index], far[index])
        lines = slice(block * height, (block + 1) * height)
        out_weights[lines, columns] = base + (out_weights[lines, columns] - weights[lines, columns])


def adam(chunk, place, rates, weights, first, second, pieces, near, far, begun):
    shape = jax.ShapeDtypeStruct(weights.shape, F32)
    rows = pl.BlockSpec((CHUNKS[chunk][1], weights.shape[1]), lambda i: (chunk, 0))
    half = CHUNKS[chunk][1] // 2
    skip = CHUNKS[0][1] // 2 if chunk else 0
    used = (2 * half, skip + 2 * half, skip + 2 * half, half, half)
    operands = (place, rates, weights, first, second, *pieces, near, far)
    return pl.pallas_call(
        functools.partial(adam_kernel, chunk),
        grid=(1,),
        out_shape=[shape] * 3,
        in_specs=[scalars(), scalars(), rows, rows, rows]
        + [pl.BlockSpec((n, p.shape[1]), lambda i: (0, 0)) for n, p in zip(used, pieces)]
        + [pl.BlockSpec(near.shape, lambda i: (0, 0, 0))] * 2
        + [pl.BlockSpec(memory_space=pl.ANY)] * len(begun),
        out_specs=[rows] * 3,
        input_output_aliases={len(operands) + i: i for i in range(len(begun))},
        compiler_params=params_of(),
        cost_estimate=COST,
        name="adam",
    )(*operands, *begun)


def pick(array, index, axis):
    return lax.dynamic_index_in_dim(array, index, axis, keepdims=False)


def local(
    hidden,
    cotangent,
    norm_gain,
    params,
    adam_first,
    adam_second,
    outer_anchor,
    outer_momentum,
    fragment,
    inner_step,
):
    tokens = hidden[0]
    cot_local = cotangent[0]
    weights = params[0]
    factor = tokens.shape[1] ** (-0.5)
    shard = lax.axis_index("shard")
    rep = lax.axis_index("rep")
    place = jnp.stack([shard // RING, shard % RING, fragment, rep]).astype(jnp.int32)

    anchor_local, moment_local = outer_anchor[0, 0], outer_momentum[0, 0]
    gain = norm_gain.reshape(1, -1)

    packed, scale = first_pack(place, tokens, gain, cot_local)
    arrived = exchange_y(packed)

    weights_half = weights.astype(BF16)
    before, after = shift_z(weights_half, 1), shift_z(weights_half, -1)

    keep, send, state = fragment_columns(place, weights, anchor_local, moment_local, scale)
    mine = jnp.concatenate([keep + swap_rep(send, 1), state])
    theirs = swap_rep(mine, 2)
    total = (mine[:8] + theirs[:8]).reshape(2, 2, 2, *keep.shape[1:])
    x_high, x_low = rep // 8, rep // 4 % 2
    total = pick(total, x_low, 1) + swap_rep(pick(total, 1 - x_low, 1), 4)
    other = swap_rep(pick(total, 1 - x_high, 0), 8)
    near, anchor_out, moment_out = outer(place, pick(total, x_high, 0), other, theirs[8:], anchor_local, moment_local)

    packed = later_pack(place, tokens, gain, scale, (near,))
    later = [packed[0]] + [shift_y(packed[k], k) for k in (1, 2, 3)]

    own_0, left, right, keep_left, keep_right = first_gradient(arrived, before, after)
    left_0, right_0 = shift_z(left, -1), shift_z(right, 1)
    own_1, left, right, next_left, next_right = later_gradient(place, later, arrived)
    left, right = join(keep_left, keep_right, left_0, right_0, left, right)
    near = jnp.concatenate([near, swap_rep(near, 8)])
    near = jnp.concatenate([near, swap_rep(near, 4)])
    far = swap_rep(near, 1)
    left_1, right_1 = shift_z(left, -1), shift_z(right, 1)
    last_left, last_right = forward(next_left, next_right, left_1, right_1)
    last_left, last_right = shift_z(last_left, -1), shift_z(last_right, 1)
    pieces = ([own_0, left_0, right_0, left_1, right_1], [own_1, left_1, right_1, last_left, last_right])

    partial = near_values(place, arrived, later, (weights_half, before, after), (own_1,))
    partial = far_values(place, partial, arrived, later, right_0, left_0)
    value_rows = values_sum(factor, [partial[0]] + [shift_y(partial[k], -k) for k in (1, 2, 3)])

    clock = inner_step.astype(F32)
    rate = PEAK_RATE * 0.5 * (1.0 + jnp.cos(math.pi * clock / HORIZON_STEPS))
    first_scale = 1.0 / (1.0 - jnp.power(FIRST_DECAY, clock))
    second_scale = 1.0 / (1.0 - jnp.power(SECOND_DECAY, clock))
    rates = jnp.stack([rate, first_scale, second_scale, jnp.full((), factor, F32)])
    begun = ()
    for chunk in range(len(CHUNKS)):
        begun = adam(
            chunk, place, rates, weights, adam_first[0], adam_second[0], pieces[chunk], near, far, begun
        )
    params_out, first_new, second_new = begun
    return (
        value_rows[None],
        params_out[None],
        first_new[None],
        second_new[None],
        anchor_out[None, None],
        moment_out[None, None],
    )


def solution(mesh):
    in_specs = (
        P("rep", "shard", None),
        P("rep", "shard", None),
        P(),
        P("rep", "shard", None),
        P("rep", "shard", None),
        P("rep", "shard", None),
        P("shard", "rep", None, None),
        P("shard", "rep", None, None),
        P(),
        P(),
    )
    out_specs = (
        P("rep", "shard", None),
        P("rep", "shard", None),
        P("rep", "shard", None),
        P("rep", "shard", None),
        P("shard", "rep", None, None),
        P("shard", "rep", None, None),
    )
    return jax.shard_map(local, mesh=mesh, in_specs=in_specs, out_specs=out_specs, check_vma=False)
```
